512 devices in a mesh: ev: 64 (over z, y), st: 8 (over x, core).
Axes of the slice: x: 4, y: 4, z: 16, core: 2. Of those that a mesh axis runs over, the one named last changes fastest.
Arguments:
- records: bfloat16 [256, 144, 3, 1024], P('ev', 'st'), may hold values from -6 to 6
- store: bfloat16 [64, 6, 144, 3, 1024], P('ev', None, 'st'), may hold values from -0.0014648438 to 0.0014648438
- taper: float32 [256], replicated, may hold values from 0.1 to 1
- candidates: int32 [256, 16], P('ev'), may hold values from 0 to 63, as said below
- node_slot: int32 [64], replicated, may hold values from 0 to 63, as said below
Outputs:
- moment: float32 [256, 16, 6], P('ev')
The draws below stay inside these ranges and needn't reach their ends.
Inputs may be any that keep to these rules, and one draw needn't show every extreme that they name: Node ids. Of the 64 candidates of the events of one index of ev (aligned blocks of 4 events), at most 2 map to the same store row (node_slot[id]), and in every block some store row is taken by exactly 2. An event may list a node more than once. `node_slot`: A permutation of 0 to 63.
All inputs are finite; a program needn't handle non-finite values.
Results may differ from the reference program's by a relative error of at most 0.005.
Values may be sent and summed in bfloat16 or wider, within the bound.
A program may use at most 64 MiB of HBM per device.

```python
import math
import jax
import jax.numpy as jnp
from jax import lax

STATIONS = 144
NSAMP = 1024
NF = 256
CAND = 16
EV_DEV = 4
NODE_DEV = 1
EVENTS = 256
NODES = 64
CAP = 2
N_EV = 64


def route_tables(key):
    ordering = jax.random.permutation(jax.random.fold_in(key, 11), NODES).astype(jnp.int32)
    inverse = jnp.argsort(ordering).astype(jnp.int32)
    slot_total = N_EV * CAP
    pair_count = EV_DEV * CAND

    def one_block(block_key):
        order_key, shuffle_key, local_key = jax.random.split(block_key, 3)
        slot_perm = jax.random.permutation(order_key, slot_total).astype(jnp.int32)
        ranking = jnp.argsort(slot_perm).astype(jnp.int32)
        first_owner = slot_perm[0] // CAP
        slot_ids = jnp.arange(slot_total, dtype=jnp.int32)
        scores = jnp.where(slot_ids // CAP == first_owner, slot_ids % CAP - CAP, ranking)
        chosen = jnp.argsort(scores).astype(jnp.int32)[:pair_count]
        chosen = chosen[jax.random.permutation(shuffle_key, pair_count)]
        owners = chosen // CAP
        local_rows = jax.random.randint(local_key, (pair_count,), 0, NODE_DEV, dtype=jnp.int32)
        return inverse[owners * NODE_DEV + local_rows]
    block_keys = jax.random.split(jax.random.fold_in(key, 12), N_EV)
    picked = jax.vmap(one_block)(block_keys).reshape(EVENTS, CAND)
    return (ordering, picked)


def draw_candidates(key, part):
    ordering, picked = route_tables(key)
    return picked.astype(jnp.int32)


def draw_node_slot(key, part):
    ordering, picked = route_tables(key)
    return ordering.astype(jnp.int32)


def shard_levels(own_key, shape, pieces, smallest, high):
    level = 1.0
    for position, shards_of in pieces:
        steps = jax.random.uniform(jax.random.fold_in(jax.random.fold_in(own_key, 6), position), (shards_of,), jnp.float32, smallest / len(pieces), high / len(pieces))
        level = level * jnp.repeat(jnp.exp(steps), shape[position] // shards_of).reshape((-1,) + (1,) * (len(shape) - 1 - position))
    return level


def noise(rng, shape, deviation, limit, cuts=(), held_as=jnp.bfloat16):
    values = jax.random.normal(rng, shape, jnp.float32) * deviation
    if len(cuts) > 0:
        values = shard_levels(rng, shape, cuts, -0.22, 0.18) * values
    return jnp.clip(values, min=-limit, max=limit).astype(held_as)


def setup_inputs(seed: int = 0) -> dict:
    splits = jax.random.split(jax.random.key(seed), 6)
    return {
        "records": noise(splits[0], (EVENTS, STATIONS, 3, NSAMP), 1.0, 6.0, ((0, 64), (1, 8))),
        "store": noise(splits[1], (NODES, 6, STATIONS, 3, NSAMP), (1.0 / (NSAMP * (STATIONS * 0.75) ** 0.5)), 0.0014648438, ((0, 64), (2, 8))),
        "taper": jnp.clip(jnp.exp(jax.random.uniform(splits[2], (NF,), jnp.float32, math.log(0.1), math.log(1.0))), 0.1, 1.0),
        "candidates": draw_candidates(jax.random.fold_in(splits[5], 71), 0),
        "node_slot": draw_node_slot(jax.random.fold_in(splits[5], 71), 0),
    }


def band_table(samples, freq_bins):
    sample_idx = jnp.arange(samples, dtype=jnp.int32)[:, None]
    bin_idx = jnp.arange(1, freq_bins + 1, dtype=jnp.int32)[None, :]
    phases = sample_idx * bin_idx % samples
    angles = phases.astype(jnp.float32) * (2.0 * math.pi / samples)
    return jnp.concatenate([jnp.cos(angles), -jnp.sin(angles)], axis=1).astype(jnp.bfloat16)

def spectra_of(traces, dft_table):
    samples = traces.shape[-1]
    result = jnp.dot(traces.reshape(-1, samples), dft_table, preferred_element_type=jnp.float32)
    return result.reshape(traces.shape[:-1] + (dft_table.shape[1],))

def trace_scale(traces):
    values = traces.astype(jnp.float32)
    return lax.rsqrt(lax.optimization_barrier(jnp.mean(values * values, axis=-1, keepdims=True)) + 1e-05) / math.sqrt(traces.shape[-1])

def solve_small(matrix, target):
    extent = target.shape[-1]
    factor = {}
    for row_at in range(extent):
        for col_at in range(row_at + 1):
            running = matrix[..., row_at, col_at]
            for mid_at in range(col_at):
                running = running - factor[row_at, mid_at] * factor[col_at, mid_at]
            if row_at == col_at:
                factor[row_at, col_at] = jnp.sqrt(running)
            else:
                factor[row_at, col_at] = running / factor[col_at, col_at]
    forward = []
    for row_at in range(extent):
        running = target[..., row_at]
        for mid_at in range(row_at):
            running = running - factor[row_at, mid_at] * forward[mid_at]
        forward.append(running / factor[row_at, row_at])
    answer = [None] * extent
    for row_at in reversed(range(extent)):
        running = forward[row_at]
        for mid_at in range(row_at + 1, extent):
            running = running - factor[mid_at, row_at] * answer[mid_at]
        answer[row_at] = running / factor[row_at, row_at]
    return jnp.stack(answer, axis=-1)

def reference(records, store, taper, candidates, node_slot):
    dft_table = band_table(records.shape[-1], taper.shape[0])
    doubled = jnp.concatenate([taper, taper])
    observed = (spectra_of(records, dft_table) * trace_scale(records)).astype(jnp.bfloat16)
    event_total = records.shape[0]
    observed_flat = observed.reshape(event_total, -1)

    def per_node(node_block):
        weighted = (spectra_of(node_block, dft_table) * doubled).astype(jnp.bfloat16).reshape(6, -1)
        gram = jnp.dot(weighted, weighted.T, preferred_element_type=jnp.float32)
        projection = jnp.dot(observed_flat, weighted.T, preferred_element_type=jnp.float32)
        return (gram, projection)
    grams, projections = lax.map(per_node, store)
    store_row = node_slot[candidates].astype(jnp.int32)
    pair_gram = grams[store_row]
    pair_proj = projections[store_row, jnp.arange(event_total, dtype=jnp.int32)[:, None]]
    return solve_small(pair_gram, pair_proj)
```

```python
import functools
import math

import jax
import jax.numpy as jnp
import numpy as np
from jax import lax
from jax.experimental import pallas as pl
from jax.experimental.pallas import tpu as pltpu
from jax.sharding import PartitionSpec as P

LANES = 128
UNITS = 8
MESH = pl.DeviceIdType.MESH


def band_table(samples, freq_bins):
    sample_idx = np.arange(samples, dtype=np.int32)[:, None]
    bin_idx = np.arange(1, freq_bins + 1, dtype=np.int32)[None, :]
    phases = sample_idx * bin_idx % samples
    angles = phases.astype(np.float32) * np.float32(2.0 * math.pi / samples)
    table = np.concatenate([np.cos(angles), -np.sin(angles)], axis=1)
    return table.astype(jnp.bfloat16)


def owner_chip(owner, core, owners, groups):
    return ((2 * owner + core) * groups) // (2 * owners)


def kernel(
    dims,
    records_hbm,
    store_hbm,
    table_hbm,
    taper_ref,
    cand_ref,
    slot_ref,
    out_ref,
    records_v,
    store_v,
    table_v,
    spectra,
    bands_a,
    bands_b,
    send_a,
    send_b,
    recv_a,
    recv_b,
    wide_a,
    wide_b,
    matrix,
    mixed,
    parts_out,
    parts_in,
    gram_slots,
    sum_slots,
    load_sem,
    gram_send,
    gram_recv,
    a_send,
    a_recv,
    b_send,
    b_recv,
    c_send,
    c_recv,
    s_send,
    s_recv,
):
    groups, members, events, elements, traces, owners, cand_count, nodes = dims
    me = lax.axis_index("ev")
    st = lax.axis_index("st")
    core = lax.rem(st, 2)
    units = traces * 4
    f32 = jnp.float32
    bf16 = jnp.bfloat16

    loads = [
        pltpu.make_async_copy(table_hbm, table_v, load_sem.at[0]),
        pltpu.make_async_copy(store_hbm, store_v, load_sem.at[1]),
        pltpu.make_async_copy(records_hbm, records_v, load_sem.at[2]),
    ]
    for load in loads:
        load.start()

    barrier = pltpu.get_barrier_semaphore()

    @pl.loop(1, members)
    def _(step):
        peer = lax.rem(st + step, members)
        pl.semaphore_signal(barrier, inc=1, device_id=(me, peer), device_id_type=MESH)

    @pl.loop(1, groups)
    def _(step):
        peer = lax.rem(me + step, groups)
        pl.semaphore_signal(barrier, inc=1, device_id=(peer, st), device_id_type=MESH)

    ranked = (2 * owners * me + groups - 1) // groups
    is_owner = (
        (ranked < 2 * owners)
        & ((ranked * groups) // (2 * owners) == me)
        & (lax.rem(ranked, 2) == core)
    )
    my_owner = ranked // 2
    first = (me * owners) // groups

    loads[0].wait()
    loads[1].wait()
    spectra[...] = jnp.dot(store_v[...], table_v[...], preferred_element_type=f32)
    for tile in range(4):
        half = (tile % 2) * LANES
        gains = taper_ref[:, half : half + LANES]
        for element in range(elements):
            block = spectra[
                element * traces : (element + 1) * traces, tile * LANES : (tile + 1) * LANES
            ]
            start = element * units + tile * traces
            bands_b[start : start + traces, :] = (block * gains).astype(bf16).astype(f32)
    pair_at = {}
    for row in range(elements):
        for col in range(row + 1):
            pair_at[row, col] = len(pair_at)
    shares = []
    for (row, col), _ in pair_at.items():
        product = (
            bands_b[row * units : (row + 1) * units, :]
            * bands_b[col * units : (col + 1) * units, :]
        )
        shares.append(jnp.sum(product, axis=0, keepdims=True))
    gram_rows = gram_slots.shape[1]
    shares.append(jnp.zeros((gram_rows - len(shares), LANES), f32))
    gram_slots[st] = jnp.concatenate(shares, axis=0)

    pl.semaphore_wait(barrier, groups + members - 2)

    def gram_copy(step):
        return pltpu.make_async_remote_copy(
            src_ref=gram_slots.at[st],
            dst_ref=gram_slots.at[st],
            send_sem=gram_send,
            recv_sem=gram_recv,
            device_id=(me, lax.rem(st + step, members)),
            device_id_type=MESH,
        )

    @pl.loop(1, members)
    def _(step):
        gram_copy(step).start()

    loads[2].wait()
    values = records_v[...].astype(f32)
    samples = values.shape[1]
    mean = jnp.sum(values * values, axis=1, keepdims=True) * (1.0 / samples)
    scale = lax.rsqrt(mean + 1e-05) * (1.0 / math.sqrt(samples))
    spectra[0 : events * traces, :] = (
        jnp.dot(records_v[...], table_v[...], preferred_element_type=f32) * scale
    )
    for tile in range(4):
        for event in range(events):
            block = spectra[
                event * traces : (event + 1) * traces, tile * LANES : (tile + 1) * LANES
            ]
            start = event * units + tile * traces
            bands_a[start : start + traces, :] = block

    def send_block(buffer, slots, owner, send_sem, recv_sem):
        chip = owner_chip(owner, core, owners, groups)

        @pl.when(chip != me)
        def _():
            pltpu.make_async_remote_copy(
                src_ref=buffer.at[owner],
                dst_ref=slots.at[me],
                send_sem=send_sem,
                recv_sem=recv_sem,
                device_id=(chip, st),
                device_id_type=MESH,
            ).start()

        @pl.when(chip == me)
        def _():
            slots[me] = buffer[owner]

    def rows_of(index, owner):
        return pl.ds(pl.multiple_of(index * units + owner * UNITS, UNITS), UNITS)

    @pl.loop(0, owners)
    def _(step):
        owner = lax.rem(first + step, owners)
        for pair in range(events // 2):
            tile = jnp.concatenate(
                [bands_a[rows_of(2 * pair, owner), :], bands_a[rows_of(2 * pair + 1, owner), :]],
                axis=0,
            )
            send_a[owner, 2 * UNITS * pair : 2 * UNITS * (pair + 1), :] = tile.astype(bf16)
        send_block(send_a, recv_a, owner, a_send, a_recv)

    others = gram_slots.at[pl.ds(0, members - 1)]
    pltpu.make_async_copy(others, others, gram_recv).wait()
    total = gram_slots[0]
    for member in range(1, members):
        total = total + gram_slots[member]
    total = jnp.broadcast_to(jnp.sum(total, axis=1, keepdims=True), total.shape)
    factor = {}
    inverse = []
    for row in range(elements):
        for col in range(row + 1):
            at = pair_at[row, col]
            running = total[at : at + 1, :]
            for mid in range(col):
                running = running - factor[row, mid] * factor[col, mid]
            if row == col:
                root = jnp.sqrt(running)
                inverse.append(1.0 / root)
            else:
                factor[row, col] = running * inverse[col]
    factor = {at: jnp.broadcast_to(value, (UNITS, LANES)) for at, value in factor.items()}
    inverse = [jnp.broadcast_to(value, (UNITS, LANES)) for value in inverse]

    @pl.loop(0, owners)
    def _(step):
        owner = lax.rem(first + step, owners)
        forward = []
        for row in range(elements):
            running = bands_b[rows_of(row, owner), :]
            for mid in range(row):
                running = running - factor[row, mid] * forward[mid]
            forward.append(running * inverse[row])
        answer = [None] * elements
        for row in reversed(range(elements)):
            running = forward[row]
            for mid in range(row + 1, elements):
                running = running - factor[mid, row] * answer[mid]
            answer[row] = running * inverse[row]
        for pair in range(elements // 2):
            tile = jnp.concatenate([answer[2 * pair], answer[2 * pair + 1]], axis=0)
            send_b[owner, 2 * UNITS * pair : 2 * UNITS * (pair + 1), :] = tile.astype(bf16)
        send_block(send_b, recv_b, owner, b_send, b_recv)

    lane_id = lax.broadcasted_iota(jnp.int32, (cand_count, LANES), 1)
    node_id = lax.broadcasted_iota(jnp.int32, (cand_count, nodes), 1)
    eye = lax.broadcasted_iota(jnp.int32, (cand_count, cand_count), 0) == (
        lax.broadcasted_iota(jnp.int32, (cand_count, cand_count), 1)
    )
    slot_values = slot_ref[...].astype(f32)
    lane_rows = []
    for event in range(events):
        wanted = jnp.where(eye, cand_ref[event : event + 1, :].astype(f32), 0.0)
        wanted = jnp.sum(wanted, axis=1, keepdims=True)
        chosen = jnp.where(node_id.astype(f32) == wanted, slot_values, 0.0)
        lane_rows.append(jnp.sum(chosen, axis=1, keepdims=True))

    def wait_all(slots, sem):
        arrived = slots.at[pl.ds(0, groups - 1)]
        pltpu.make_async_copy(arrived, arrived, sem).wait()

    @pl.when(is_owner)
    def _():
        for slots, wide, sem, count, base in (
            (recv_a, wide_a, a_recv, events, 0),
            (recv_b, wide_b, b_recv, elements, events),
        ):
            wait_all(slots, sem)
            wide[...] = slots[...].astype(f32).reshape(wide.shape)
            stride = count * UNITS

            @pl.loop(0, UNITS)
            def _(unit):
                lanes = pl.ds(pl.multiple_of(unit * LANES, LANES), LANES)
                for row in range(count):
                    picked = wide[pl.ds(row * UNITS + unit, groups, stride=stride), :]
                    at = (base + row) * groups
                    matrix[at : at + groups, lanes] = picked.astype(bf16)

        products = lax.dot_general(
            matrix[0 : events * groups, :],
            matrix[events * groups : (events + elements) * groups, :],
            (((1,), (1,)), ((), ())),
            preferred_element_type=f32,
        )
        mixed[...] = jnp.zeros_like(mixed)
        for tile in range(elements * nodes // LANES):
            for event in range(events):
                mixed[pl.ds(tile * events + event, groups, stride=16), :] = products[
                    event * groups : (event + 1) * groups, tile * LANES : (tile + 1) * LANES
                ]
        parts_out[...] = mixed[...].astype(bf16).reshape(parts_out.shape)

        @pl.loop(1, groups)
        def _(step):
            peer = lax.rem(me + step, groups)
            pltpu.make_async_remote_copy(
                src_ref=parts_out.at[peer],
                dst_ref=parts_in.at[my_owner],
                send_sem=c_send,
                recv_sem=c_recv,
                device_id=(peer, st),
                device_id_type=MESH,
            ).start()

        parts_in[my_owner] = parts_out[me]

    @pl.when(is_owner)
    def _():
        arrived = parts_in.at[pl.ds(0, owners - 1)]
        pltpu.make_async_copy(arrived, arrived, c_recv).wait()

    @pl.when(jnp.logical_not(is_owner))
    def _():
        arrived = parts_in.at[pl.ds(0, owners)]
        pltpu.make_async_copy(arrived, arrived, c_recv).wait()

    sum_slots[st] = jnp.sum(parts_in[...].astype(f32), axis=0)

    @pl.loop(1, members)
    def _(step):
        pltpu.make_async_remote_copy(
            src_ref=sum_slots.at[st],
            dst_ref=sum_slots.at[st],
            send_sem=s_send,
            recv_sem=s_recv,
            device_id=(me, lax.rem(st + step, members)),
            device_id_type=MESH,
        ).start()

    others = sum_slots.at[pl.ds(0, members - 1)]
    pltpu.make_async_copy(others, others, s_recv).wait()
    moments = sum_slots[0]
    for member in range(1, members):
        moments = moments + sum_slots[member]

    lane_f = lane_id.astype(f32)
    out_lane = lax.broadcasted_iota(jnp.int32, (cand_count, elements), 1)
    per_tile = LANES // nodes
    for event in range(events):
        result = jnp.zeros((cand_count, elements), f32)
        for element in range(elements):
            tile, part = element // per_tile, element % per_tile
            line = moments[tile * events + event : tile * events + event + 1, :]
            mask = lane_f == lane_rows[event] + float(part * nodes)
            value = jnp.sum(jnp.where(mask, line, 0.0), axis=1, keepdims=True)
            result = jnp.where(out_lane == element, value, result)
        out_ref[event] = result

    pltpu.make_async_copy(others, others, s_send).wait()
    sent = gram_slots.at[pl.ds(0, members - 1)]
    pltpu.make_async_copy(sent, sent, gram_send).wait()

    @pl.when(is_owner)
    def _():
        for buffer, sem in ((send_a, a_send), (send_b, b_send), (parts_out, c_send)):
            sent = buffer.at[pl.ds(0, buffer.shape[0] - 1)]
            pltpu.make_async_copy(sent, sent, sem).wait()

    @pl.when(jnp.logical_not(is_owner))
    def _():
        for buffer, sem in ((send_a, a_send), (send_b, b_send)):
            pltpu.make_async_copy(buffer, buffer, sem).wait()


def shards(records, store, taper, candidates, node_slot):
    groups, members = lax.axis_size("ev"), lax.axis_size("st")
    events, stations, comps, samples = records.shape
    elements = store.shape[1]
    traces = stations * comps
    bins = 2 * taper.shape[0]
    owners = traces * bins // (UNITS * LANES)
    cand_count = candidates.shape[1]
    nodes = node_slot.shape[0]
    dims = (groups, members, events, elements, traces, owners, cand_count, nodes)
    units = traces * (bins // LANES)
    f32, bf16 = jnp.float32, jnp.bfloat16
    table = jnp.asarray(band_table(samples, taper.shape[0]))
    anywhere = pl.BlockSpec(memory_space=pl.ANY)
    vmem = pl.BlockSpec(memory_space=pltpu.VMEM)
    rows_a, rows_b = events * UNITS, elements * UNITS
    return pl.pallas_call(
        functools.partial(kernel, dims),
        out_shape=jax.ShapeDtypeStruct((events, cand_count, elements), f32),
        in_specs=[anywhere] * 3 + [vmem] * 3,
        out_specs=vmem,
        scratch_shapes=[
            pltpu.VMEM((events * traces, samples), bf16),
            pltpu.VMEM((elements * traces, samples), bf16),
            pltpu.VMEM((samples, bins), bf16),
            pltpu.VMEM((elements * traces, bins), f32),
            pltpu.VMEM((events * units, LANES), f32),
            pltpu.VMEM((elements * units, LANES), f32),
            pltpu.VMEM((owners, rows_a, LANES), bf16),
            pltpu.VMEM((owners, rows_b, LANES), bf16),
            pltpu.VMEM((groups, rows_a, LANES), bf16),
            pltpu.VMEM((groups, rows_b, LANES), bf16),
            pltpu.VMEM((groups * rows_a, LANES), f32),
            pltpu.VMEM((groups * rows_b, LANES), f32),
            pltpu.VMEM(((events + elements) * groups, UNITS * LANES), bf16),
            pltpu.VMEM((groups * 16, LANES), f32),
            pltpu.VMEM((groups, 16, LANES), bf16),
            pltpu.VMEM((owners, 16, LANES), bf16),
            pltpu.VMEM((members, 24, LANES), f32),
            pltpu.VMEM((members, 16, LANES), f32),
            pltpu.SemaphoreType.DMA((3,)),
        ]
        + [pltpu.SemaphoreType.DMA] * 10,
        compiler_params=pltpu.CompilerParams(
            collective_id=0, has_side_effects=True, vmem_limit_bytes=40 * 1024 * 1024
        ),
    )(
        records.reshape(events * traces, samples),
        store.reshape(elements * traces, samples),
        table,
        taper.reshape(1, -1),
        candidates,
        node_slot.reshape(1, -1),
    )


def solution(mesh):
    return jax.shard_map(
        shards,
        mesh=mesh,
        in_specs=(
            P("ev", "st", None, None),
            P("ev", None, "st", None, None),
            P(),
            P("ev", None),
            P(),
        ),
        out_specs=P("ev", None, None),
        check_vma=False,
    )
```

```python
import functools
import math

import jax
import jax.numpy as jnp
import numpy as np
from jax import lax
from jax.experimental import pallas as pl
from jax.experimental.pallas import tpu as pltpu
from jax.sharding import PartitionSpec as P

LANES = 128
UNITS = 8
CHUNKS = 4
MESH = pl.DeviceIdType.MESH


def band_table(samples, freq_bins):
    sample_idx = np.arange(samples, dtype=np.int32)[:, None]
    bin_idx = np.arange(1, freq_bins + 1, dtype=np.int32)[None, :]
    phases = sample_idx * bin_idx % samples
    angles = phases.astype(np.float32) * np.float32(2.0 * math.pi / samples)
    table = np.concatenate([np.cos(angles), -np.sin(angles)], axis=1)
    return table.astype(jnp.bfloat16)


def owner_chip(owner, core, owners, groups):
    return ((2 * owner + core) * groups) // (2 * owners)


def around(step, count):
    step = count - 1 - step
    half = (step + 1) // 2
    return jnp.where(lax.rem(step, 2) == 0, half, lax.rem(count - half, count))


def far_rank(offset, count):
    half = count // 2
    return jnp.where(offset < half, 2 * (half - offset) - 1, 2 * (offset - half))


def far_offset(rank, count):
    half = count // 2
    return jnp.where(lax.rem(rank, 2) == 0, half + rank // 2, half - (rank + 1) // 2)


def kernel(
    dims,
    records_hbm,
    store_hbm,
    table_hbm,
    taper_ref,
    cand_ref,
    slot_ref,
    out_ref,
    records_v,
    store_v,
    table_v,
    spectra,
    bands_a,
    bands_b,
    send_a,
    send_b,
    recv_a,
    recv_b,
    wide_a,
    wide_b,
    matrix_a,
    matrix_b,
    mixed,
    parts_out,
    parts_in,
    gram_slots,
    sum_slots,
    load_sem,
    gram_send,
    gram_recv,
    a_send,
    a_recv,
    b_send,
    b_recv,
    c_send,
    c_recv,
    s_send,
    s_recv,
):
    groups, members, events, elements, traces, owners, cand_count, nodes = dims
    me = lax.axis_index("ev")
    st = lax.axis_index("st")
    core = lax.rem(st, 2)
    units = traces * 4
    f32 = jnp.float32
    bf16 = jnp.bfloat16

    loads = [
        pltpu.make_async_copy(table_hbm, table_v, load_sem.at[0]),
        pltpu.make_async_copy(store_hbm, store_v, load_sem.at[1]),
        pltpu.make_async_copy(records_hbm, records_v, load_sem.at[2]),
    ]
    for load in loads:
        load.start()

    barrier = pltpu.get_barrier_semaphore()

    @pl.loop(1, members)
    def _(step):
        peer = lax.rem(st + step, members)
        pl.semaphore_signal(barrier, inc=1, device_id=(me, peer), device_id_type=MESH)

    @pl.loop(1, groups)
    def _(step):
        peer = lax.rem(me + step, groups)
        pl.semaphore_signal(barrier, inc=1, device_id=(peer, st), device_id_type=MESH)

    ranked = (2 * owners * me + groups - 1) // groups
    is_owner = (
        (ranked < 2 * owners)
        & ((ranked * groups) // (2 * owners) == me)
        & (lax.rem(ranked, 2) == core)
    )
    my_owner = ranked // 2
    first = (me * owners) // groups

    loads[0].wait()
    loads[1].wait()
    height = elements * traces

    def by_tiles(values):
        for tile in range(4):
            start = tile * height
            spectra[start : start + values.shape[0], :] = values[
                :, tile * LANES : (tile + 1) * LANES
            ]

    by_tiles(jnp.dot(store_v[...], table_v[...], preferred_element_type=f32))
    for tile in range(4):
        half = (tile % 2) * LANES
        gains = taper_ref[:, half : half + LANES]
        for element in range(elements):
            source = tile * height + element * traces
            block = spectra[source : source + traces, :]
            start = element * units + tile * traces
            bands_b[start : start + traces, :] = (block * gains).astype(bf16).astype(f32)
    pair_at = {}
    for row in range(elements):
        for col in range(row + 1):
            pair_at[row, col] = len(pair_at)
    shares = []
    for (row, col), _ in pair_at.items():
        product = (
            bands_b[row * units : (row + 1) * units, :]
            * bands_b[col * units : (col + 1) * units, :]
        )
        shares.append(jnp.sum(product, axis=0, keepdims=True))
    gram_rows = gram_slots.shape[1]
    shares.append(jnp.zeros((gram_rows - len(shares), LANES), f32))
    gram_slots[st] = jnp.concatenate(shares, axis=0)

    pl.semaphore_wait(barrier, groups + members - 2)

    def gram_copy(step):
        return pltpu.make_async_remote_copy(
            src_ref=gram_slots.at[st],
            dst_ref=gram_slots.at[st],
            send_sem=gram_send,
            recv_sem=gram_recv,
            device_id=(me, lax.rem(st + step, members)),
            device_id_type=MESH,
        )

    @pl.loop(1, members)
    def _(step):
        gram_copy(step).start()

    loads[2].wait()
    values = records_v[...].astype(f32)
    samples = values.shape[1]
    mean = jnp.sum(values * values, axis=1, keepdims=True) * (1.0 / samples)
    scale = lax.rsqrt(mean + 1e-05) * (1.0 / math.sqrt(samples))
    by_tiles(jnp.dot(records_v[...], table_v[...], preferred_element_type=f32) * scale)
    for tile in range(4):
        for event in range(events):
            block = spectra[pl.ds(tile * height + event, traces, stride=events), :]
            start = event * units + tile * traces
            bands_a[start : start + traces, :] = block

    def send_block(buffer, slots, owner, slot, send_sem, recv_sem):
        chip = owner_chip(owner, core, owners, groups)

        @pl.when(chip != me)
        def _():
            pltpu.make_async_remote_copy(
                src_ref=buffer.at[owner],
                dst_ref=slots.at[slot],
                send_sem=send_sem,
                recv_sem=recv_sem,
                device_id=(chip, st),
                device_id_type=MESH,
            ).start()

        @pl.when(chip == me)
        def _():
            slots[slot] = buffer[owner]

    def rows_of(index, owner):
        return pl.ds(pl.multiple_of(index * units + owner * UNITS, UNITS), UNITS)

    span = groups // CHUNKS

    def send_observed(step):
        owner = lax.rem(first + around(step, owners), owners)
        for pair in range(events // 2):
            tile = jnp.concatenate(
                [bands_a[rows_of(2 * pair, owner), :], bands_a[rows_of(2 * pair + 1, owner), :]],
                axis=0,
            )
            send_a[owner, 2 * UNITS * pair : 2 * UNITS * (pair + 1), :] = tile.astype(bf16)
        offset = lax.rem(owner_chip(owner, core, owners, groups) - me + groups, groups)
        rank = far_rank(offset, groups)
        send_block(send_a, recv_a, owner, rank, a_send, a_recv.at[rank // span])

    early = owners // 2

    @pl.loop(0, early)
    def _(step):
        send_observed(step)

    others = gram_slots.at[pl.ds(0, members - 1)]
    pltpu.make_async_copy(others, others, gram_recv).wait()
    total = gram_slots[0]
    for member in range(1, members):
        total = total + gram_slots[member]
    total = jnp.broadcast_to(jnp.sum(total, axis=1, keepdims=True), total.shape)
    factor = {}
    inverse = []
    for row in range(elements):
        for col in range(row + 1):
            at = pair_at[row, col]
            running = total[at : at + 1, :]
            for mid in range(col):
                running = running - factor[row, mid] * factor[col, mid]
            if row == col:
                root = jnp.sqrt(running)
                inverse.append(1.0 / root)
            else:
                factor[row, col] = running * inverse[col]
    factor = {at: jnp.broadcast_to(value, (UNITS, LANES)) for at, value in factor.items()}
    inverse = [jnp.broadcast_to(value, (UNITS, LANES)) for value in inverse]

    @pl.loop(0, owners)
    def _(step):
        owner = lax.rem(first + around(step, owners), owners)
        forward = []
        for row in range(elements):
            running = bands_b[rows_of(row, owner), :]
            for mid in range(row):
                running = running - factor[row, mid] * forward[mid]
            forward.append(running * inverse[row])
        answer = [None] * elements
        for row in reversed(range(elements)):
            running = forward[row]
            for mid in range(row + 1, elements):
                running = running - factor[mid, row] * answer[mid]
            answer[row] = running * inverse[row]
        for pair in range(elements // 2):
            tile = jnp.concatenate([answer[2 * pair], answer[2 * pair + 1]], axis=0)
            send_b[owner, 2 * UNITS * pair : 2 * UNITS * (pair + 1), :] = tile.astype(bf16)
        send_block(send_b, recv_b, owner, me, b_send, b_recv)

    @pl.loop(early, owners)
    def _(step):
        send_observed(step)

    lane_id = lax.broadcasted_iota(jnp.int32, (cand_count, LANES), 1)
    node_id = lax.broadcasted_iota(jnp.int32, (cand_count, nodes), 1)
    eye = lax.broadcasted_iota(jnp.int32, (cand_count, cand_count), 0) == (
        lax.broadcasted_iota(jnp.int32, (cand_count, cand_count), 1)
    )
    slot_values = slot_ref[...].astype(f32)
    lane_rows = []
    for event in range(events):
        wanted = jnp.where(eye, cand_ref[event : event + 1, :].astype(f32), 0.0)
        wanted = jnp.sum(wanted, axis=1, keepdims=True)
        chosen = jnp.where(node_id.astype(f32) == wanted, slot_values, 0.0)
        lane_rows.append(jnp.sum(chosen, axis=1, keepdims=True))

    def spread(wide, target, count, height):
        @pl.loop(0, UNITS)
        def _(unit):
            lanes = pl.ds(pl.multiple_of(unit * LANES, LANES), LANES)
            for row in range(count):
                picked = wide[pl.ds(row * UNITS + unit, height, stride=count * UNITS), :]
                target[row * height : (row + 1) * height, lanes] = picked.astype(bf16)

    @pl.when(is_owner)
    def _():
        mixed[...] = jnp.zeros_like(mixed)
        arrived = recv_b.at[pl.ds(0, groups - 1)]
        pltpu.make_async_copy(arrived, arrived, b_recv).wait()
        wide_b[...] = recv_b[...].astype(f32).reshape(wide_b.shape)
        spread(wide_b, matrix_b, elements, groups)
        for chunk in range(CHUNKS):
            start, stop = chunk * span, (chunk + 1) * span
            remote = min(stop, groups - 1)
            arrived = recv_a.at[pl.ds(start, remote - start)]
            pltpu.make_async_copy(arrived, arrived, a_recv.at[chunk]).wait()
            wide_a[...] = recv_a[start:stop].astype(f32).reshape(wide_a.shape)
            spread(wide_a, matrix_a, events, span)
            products = lax.dot_general(
                matrix_a[...],
                matrix_b[...],
                (((1,), (1,)), ((), ())),
                preferred_element_type=f32,
            )
            for tile in range(elements * nodes // LANES):
                for event in range(events):
                    mixed[pl.ds(tile * events + event, span, stride=16), :] = products[
                        event * span : (event + 1) * span, tile * LANES : (tile + 1) * LANES
                    ]
            parts_out[start:stop] = mixed[...].astype(bf16).reshape(span, 16, LANES)

            @pl.loop(start, remote)
            def _(rank):
                peer = lax.rem(me - far_offset(rank, groups) + groups, groups)
                pltpu.make_async_remote_copy(
                    src_ref=parts_out.at[rank],
                    dst_ref=parts_in.at[my_owner],
                    send_sem=c_send,
                    recv_sem=c_recv,
                    device_id=(peer, st),
                    device_id_type=MESH,
                ).start()

        parts_in[my_owner] = parts_out[groups - 1]

    @pl.when(is_owner)
    def _():
        arrived = parts_in.at[pl.ds(0, owners - 1)]
        pltpu.make_async_copy(arrived, arrived, c_recv).wait()

    @pl.when(jnp.logical_not(is_owner))
    def _():
        arrived = parts_in.at[pl.ds(0, owners)]
        pltpu.make_async_copy(arrived, arrived, c_recv).wait()

    sum_slots[st] = jnp.sum(parts_in[...].astype(f32), axis=0)

    @pl.loop(1, members)
    def _(step):
        pltpu.make_async_remote_copy(
            src_ref=sum_slots.at[st],
            dst_ref=sum_slots.at[st],
            send_sem=s_send,
            recv_sem=s_recv,
            device_id=(me, lax.rem(st + step, members)),
            device_id_type=MESH,
        ).start()

    others = sum_slots.at[pl.ds(0, members - 1)]
    pltpu.make_async_copy(others, others, s_recv).wait()
    moments = sum_slots[0]
    for member in range(1, members):
        moments = moments + sum_slots[member]

    lane_f = lane_id.astype(f32)
    out_lane = lax.broadcasted_iota(jnp.int32, (cand_count, elements), 1)
    per_tile = LANES // nodes
    for event in range(events):
        result = jnp.zeros((cand_count, elements), f32)
        for element in range(elements):
            tile, part = element // per_tile, element % per_tile
            line = moments[tile * events + event : tile * events + event + 1, :]
            mask = lane_f == lane_rows[event] + float(part * nodes)
            value = jnp.sum(jnp.where(mask, line, 0.0), axis=1, keepdims=True)
            result = jnp.where(out_lane == element, value, result)
        out_ref[event] = result

    pltpu.make_async_copy(others, others, s_send).wait()
    sent = gram_slots.at[pl.ds(0, members - 1)]
    pltpu.make_async_copy(sent, sent, gram_send).wait()

    @pl.when(is_owner)
    def _():
        for buffer, sem in ((send_a, a_send), (send_b, b_send), (parts_out, c_send)):
            sent = buffer.at[pl.ds(0, buffer.shape[0] - 1)]
            pltpu.make_async_copy(sent, sent, sem).wait()

    @pl.when(jnp.logical_not(is_owner))
    def _():
        for buffer, sem in ((send_a, a_send), (send_b, b_send)):
            pltpu.make_async_copy(buffer, buffer, sem).wait()


def shards(records, store, taper, candidates, node_slot):
    groups, members = lax.axis_size("ev"), lax.axis_size("st")
    events, stations, comps, samples = records.shape
    elements = store.shape[1]
    traces = stations * comps
    bins = 2 * taper.shape[0]
    owners = traces * bins // (UNITS * LANES)
    cand_count = candidates.shape[1]
    nodes = node_slot.shape[0]
    dims = (groups, members, events, elements, traces, owners, cand_count, nodes)
    units = traces * (bins // LANES)
    f32, bf16 = jnp.float32, jnp.bfloat16
    table = jnp.asarray(band_table(samples, taper.shape[0]))
    anywhere = pl.BlockSpec(memory_space=pl.ANY)
    vmem = pl.BlockSpec(memory_space=pltpu.VMEM)
    rows_a, rows_b = events * UNITS, elements * UNITS
    return pl.pallas_call(
        functools.partial(kernel, dims),
        out_shape=jax.ShapeDtypeStruct((events, cand_count, elements), f32),
        in_specs=[anywhere] * 3 + [vmem] * 3,
        out_specs=vmem,
        scratch_shapes=[
            pltpu.VMEM((events * traces, samples), bf16),
            pltpu.VMEM((elements * traces, samples), bf16),
            pltpu.VMEM((samples, bins), bf16),
            pltpu.VMEM((elements * traces * (bins // LANES), LANES), f32),
            pltpu.VMEM((events * units, LANES), f32),
            pltpu.VMEM((elements * units, LANES), f32),
            pltpu.VMEM((owners, rows_a, LANES), bf16),
            pltpu.VMEM((owners, rows_b, LANES), bf16),
            pltpu.VMEM((groups, rows_a, LANES), bf16),
            pltpu.VMEM((groups, rows_b, LANES), bf16),
            pltpu.VMEM((groups // CHUNKS * rows_a, LANES), f32),
            pltpu.VMEM((groups * rows_b, LANES), f32),
            pltpu.VMEM((groups // CHUNKS * events, UNITS * LANES), bf16),
            pltpu.VMEM((elements * groups, UNITS * LANES), bf16),
            pltpu.VMEM((groups // CHUNKS * 16, LANES), f32),
            pltpu.VMEM((groups, 16, LANES), bf16),
            pltpu.VMEM((owners, 16, LANES), bf16),
            pltpu.VMEM((members, 24, LANES), f32),
            pltpu.VMEM((members, 16, LANES), f32),
            pltpu.SemaphoreType.DMA((3,)),
        ]
        + [pltpu.SemaphoreType.DMA] * 3
        + [pltpu.SemaphoreType.DMA((CHUNKS,))]
        + [pltpu.SemaphoreType.DMA] * 6,
        compiler_params=pltpu.CompilerParams(
            collective_id=0, has_side_effects=True, vmem_limit_bytes=40 * 1024 * 1024
        ),
    )(
        records.transpose(1, 2, 0, 3).reshape(traces * events, samples),
        store.reshape(elements * traces, samples),
        table,
        taper.reshape(1, -1),
        candidates,
        node_slot.reshape(1, -1),
    )


def solution(mesh):
    return jax.shard_map(
        shards,
        mesh=mesh,
        in_specs=(
            P("ev", "st", None, None),
            P("ev", None, "st", None, None),
            P(),
            P("ev", None),
            P(),
        ),
        out_specs=P("ev", None, None),
        check_vma=False,
    )
```

```python
import functools
import math

import jax
import jax.numpy as jnp
import numpy as np
from jax import lax
from jax.experimental import pallas as pl
from jax.experimental.pallas import tpu as pltpu
from jax.sharding import PartitionSpec as P

LANES = 128
UNITS = 8
CHUNKS = 4
MESH = pl.DeviceIdType.MESH


def band_table(samples, freq_bins):
    sample_idx = np.arange(samples, dtype=np.int32)[:, None]
    bin_idx = np.arange(1, freq_bins + 1, dtype=np.int32)[None, :]
    phases = sample_idx * bin_idx % samples
    angles = phases.astype(np.float32) * np.float32(2.0 * math.pi / samples)
    table = np.concatenate([np.cos(angles), -np.sin(angles)], axis=1)
    return table.astype(jnp.bfloat16)


def owner_chip(owner, core, owners, groups):
    return ((2 * owner + core) * groups) // (2 * owners)


def around(step, count):
    step = count - 1 - step
    half = (step + 1) // 2
    return jnp.where(lax.rem(step, 2) == 0, half, lax.rem(count - half, count))


def far_rank(offset, count):
    half = count // 2
    return jnp.where(offset < half, 2 * (half - offset) - 1, 2 * (offset - half))


def far_offset(rank, count):
    half = count // 2
    return jnp.where(lax.rem(rank, 2) == 0, half + rank // 2, half - (rank + 1) // 2)


def kernel(
    dims,
    records_hbm,
    store_hbm,
    table_hbm,
    taper_hbm,
    cand_hbm,
    slot_hbm,
    out_ref,
    records_v,
    store_v,
    table_v,
    taper_ref,
    cand_ref,
    slot_ref,
    spectra,
    bands_a,
    bands_b,
    send_a,
    send_b,
    recv_a,
    recv_b,
    wide_a,
    wide_b,
    matrix_a,
    matrix_b,
    mixed,
    parts_out,
    parts_in,
    gram_slots,
    sum_slots,
    load_sem,
    gram_send,
    gram_recv,
    a_send,
    a_recv,
    b_send,
    b_recv,
    c_send,
    c_recv,
    s_send,
    s_recv,
):
    groups, members, events, elements, traces, owners, cand_count, nodes = dims
    me = lax.axis_index("ev")
    st = lax.axis_index("st")
    core = lax.rem(st, 2)
    units = traces * 4
    f32 = jnp.float32
    bf16 = jnp.bfloat16

    loads = [
        pltpu.make_async_copy(table_hbm, table_v, load_sem.at[0]),
        pltpu.make_async_copy(store_hbm, store_v, load_sem.at[1]),
        pltpu.make_async_copy(records_hbm, records_v, load_sem.at[2]),
        pltpu.make_async_copy(taper_hbm, taper_ref, load_sem.at[3]),
        pltpu.make_async_copy(cand_hbm, cand_ref, load_sem.at[4]),
        pltpu.make_async_copy(slot_hbm, slot_ref, load_sem.at[5]),
    ]
    for load in loads:
        load.start()

    barrier = pltpu.get_barrier_semaphore()

    def shifted(index, offset, count):
        total = index + offset
        return jnp.where(total >= count, total - count, total)

    for offset in sorted(range(1, groups), key=lambda at: abs(at - groups // 2)):
        peer = shifted(me, offset, groups)
        pl.semaphore_signal(barrier, inc=1, device_id=(peer, st), device_id_type=MESH)
    for offset in range(1, members):
        peer = shifted(st, offset, members)
        pl.semaphore_signal(barrier, inc=1, device_id=(me, peer), device_id_type=MESH)

    ranked = (2 * owners * me + groups - 1) // groups
    is_owner = (
        (ranked < 2 * owners)
        & ((ranked * groups) // (2 * owners) == me)
        & (lax.rem(ranked, 2) == core)
    )
    my_owner = ranked // 2
    first = (me * owners) // groups

    loads[0].wait()
    loads[1].wait()
    loads[3].wait()
    height = elements * traces

    def by_tiles(values):
        for tile in range(4):
            start = tile * height
            spectra[start : start + values.shape[0], :] = values[
                :, tile * LANES : (tile + 1) * LANES
            ]

    samples = table_v.shape[0]
    rows = store_v[...].reshape(elements * traces, samples)
    by_tiles(jnp.dot(rows, table_v[...], preferred_element_type=f32))
    for tile in range(4):
        half = (tile % 2) * LANES
        gains = taper_ref[:, half : half + LANES]
        for element in range(elements):
            source = tile * height + element * traces
            block = spectra[source : source + traces, :]
            start = element * units + tile * traces
            bands_b[start : start + traces, :] = (block * gains).astype(bf16).astype(f32)
    pair_at = {}
    for row in range(elements):
        for col in range(row + 1):
            pair_at[row, col] = len(pair_at)
    shares = []
    for (row, col), _ in pair_at.items():
        product = (
            bands_b[row * units : (row + 1) * units, :]
            * bands_b[col * units : (col + 1) * units, :]
        )
        shares.append(jnp.sum(product, axis=0, keepdims=True))
    gram_rows = gram_slots.shape[1]
    shares.append(jnp.zeros((gram_rows - len(shares), LANES), f32))
    gram_slots[st] = jnp.concatenate(shares, axis=0)

    loads[2].wait()
    rows = records_v[...].reshape(traces * events, samples)
    values = rows.astype(f32)
    mean = jnp.sum(values * values, axis=1, keepdims=True) * (1.0 / samples)
    scale = lax.rsqrt(mean + 1e-05) * (1.0 / math.sqrt(samples))
    by_tiles(jnp.dot(rows, table_v[...], preferred_element_type=f32) * scale)
    for tile in range(4):
        for event in range(events):
            block = spectra[pl.ds(tile * height + event, traces, stride=events), :]
            start = event * units + tile * traces
            bands_a[start : start + traces, :] = block

    def rows_of(index, owner):
        return pl.ds(pl.multiple_of(index * units + owner * UNITS, UNITS), UNITS)

    @pl.loop(0, owners)
    def _(owner):
        for pair in range(events // 2):
            tile = jnp.concatenate(
                [bands_a[rows_of(2 * pair, owner), :], bands_a[rows_of(2 * pair + 1, owner), :]],
                axis=0,
            )
            send_a[owner, 2 * UNITS * pair : 2 * UNITS * (pair + 1), :] = tile.astype(bf16)

    pl.semaphore_wait(barrier, groups + members - 2)

    def gram_copy(step):
        return pltpu.make_async_remote_copy(
            src_ref=gram_slots.at[st],
            dst_ref=gram_slots.at[st],
            send_sem=gram_send,
            recv_sem=gram_recv,
            device_id=(me, lax.rem(st + step, members)),
            device_id_type=MESH,
        )

    @pl.loop(1, members)
    def _(step):
        gram_copy(step).start()

    def send_block(buffer, slots, owner, slot, send_sem, recv_sem):
        chip = owner_chip(owner, core, owners, groups)

        @pl.when(chip != me)
        def _():
            pltpu.make_async_remote_copy(
                src_ref=buffer.at[owner],
                dst_ref=slots.at[slot],
                send_sem=send_sem,
                recv_sem=recv_sem,
                device_id=(chip, st),
                device_id_type=MESH,
            ).start()

        @pl.when(chip == me)
        def _():
            slots[slot] = buffer[owner]

    span = groups // CHUNKS

    def send_observed(step):
        owner = lax.rem(first + around(step, owners), owners)
        offset = lax.rem(owner_chip(owner, core, owners, groups) - me + groups, groups)
        rank = far_rank(offset, groups)
        send_block(send_a, recv_a, owner, rank, a_send, a_recv.at[rank // span])

    early = owners // 2

    @pl.loop(0, early)
    def _(step):
        send_observed(step)

    others = gram_slots.at[pl.ds(0, members - 1)]
    pltpu.make_async_copy(others, others, gram_recv).wait()
    total = gram_slots[0]
    for member in range(1, members):
        total = total + gram_slots[member]
    total = jnp.broadcast_to(jnp.sum(total, axis=1, keepdims=True), total.shape)
    factor = {}
    inverse = []
    for row in range(elements):
        for col in range(row + 1):
            at = pair_at[row, col]
            running = total[at : at + 1, :]
            for mid in range(col):
                running = running - factor[row, mid] * factor[col, mid]
            if row == col:
                root = jnp.sqrt(running)
                inverse.append(1.0 / root)
            else:
                factor[row, col] = running * inverse[col]
    factor = {at: jnp.broadcast_to(value, (UNITS, LANES)) for at, value in factor.items()}
    inverse = [jnp.broadcast_to(value, (UNITS, LANES)) for value in inverse]

    @pl.loop(0, owners)
    def _(step):
        owner = lax.rem(first + around(step, owners), owners)
        forward = []
        for row in range(elements):
            running = bands_b[rows_of(row, owner), :]
            for mid in range(row):
                running = running - factor[row, mid] * forward[mid]
            forward.append(running * inverse[row])
        answer = [None] * elements
        for row in reversed(range(elements)):
            running = forward[row]
            for mid in range(row + 1, elements):
                running = running - factor[mid, row] * answer[mid]
            answer[row] = running * inverse[row]
        for pair in range(elements // 2):
            tile = jnp.concatenate([answer[2 * pair], answer[2 * pair + 1]], axis=0)
            send_b[owner, 2 * UNITS * pair : 2 * UNITS * (pair + 1), :] = tile.astype(bf16)
        send_block(send_b, recv_b, owner, me, b_send, b_recv)

    @pl.loop(early, owners)
    def _(step):
        send_observed(step)

    loads[4].wait()
    loads[5].wait()
    lane_id = lax.broadcasted_iota(jnp.int32, (cand_count, LANES), 1)
    node_id = lax.broadcasted_iota(jnp.int32, (cand_count, nodes), 1)
    eye = lax.broadcasted_iota(jnp.int32, (cand_count, cand_count), 0) == (
        lax.broadcasted_iota(jnp.int32, (cand_count, cand_count), 1)
    )
    slot_values = slot_ref[...].astype(f32)
    lane_rows = []
    for event in range(events):
        wanted = jnp.where(eye, cand_ref[event : event + 1, :].astype(f32), 0.0)
        wanted = jnp.sum(wanted, axis=1, keepdims=True)
        chosen = jnp.where(node_id.astype(f32) == wanted, slot_values, 0.0)
        lane_rows.append(jnp.sum(chosen, axis=1, keepdims=True))

    def spread(wide, target, count, height):
        @pl.loop(0, UNITS)
        def _(unit):
            lanes = pl.ds(pl.multiple_of(unit * LANES, LANES), LANES)
            for row in range(count):
                picked = wide[pl.ds(row * UNITS + unit, height, stride=count * UNITS), :]
                target[row * height : (row + 1) * height, lanes] = picked.astype(bf16)

    @pl.when(is_owner)
    def _():
        mixed[...] = jnp.zeros_like(mixed)
        arrived = recv_b.at[pl.ds(0, groups - 1)]
        pltpu.make_async_copy(arrived, arrived, b_recv).wait()
        wide_b[...] = recv_b[...].astype(f32).reshape(wide_b.shape)
        spread(wide_b, matrix_b, elements, groups)
        for chunk in range(CHUNKS):
            start, stop = chunk * span, (chunk + 1) * span
            remote = min(stop, groups - 1)
            arrived = recv_a.at[pl.ds(start, remote - start)]
            pltpu.make_async_copy(arrived, arrived, a_recv.at[chunk]).wait()
            wide_a[...] = recv_a[start:stop].astype(f32).reshape(wide_a.shape)
            spread(wide_a, matrix_a, events, span)
            products = lax.dot_general(
                matrix_a[...],
                matrix_b[...],
                (((1,), (1,)), ((), ())),
                preferred_element_type=f32,
            )
            for tile in range(elements * nodes // LANES):
                for event in range(events):
                    mixed[pl.ds(tile * events + event, span, stride=16), :] = products[
                        event * span : (event + 1) * span, tile * LANES : (tile + 1) * LANES
                    ]
            parts_out[start:stop] = mixed[...].astype(bf16).reshape(span, 16, LANES)

            @pl.loop(start, remote)
            def _(rank):
                peer = lax.rem(me - far_offset(rank, groups) + groups, groups)
                pltpu.make_async_remote_copy(
                    src_ref=parts_out.at[rank],
                    dst_ref=parts_in.at[my_owner],
                    send_sem=c_send,
                    recv_sem=c_recv,
                    device_id=(peer, st),
                    device_id_type=MESH,
                ).start()

        parts_in[my_owner] = parts_out[groups - 1]

    @pl.when(is_owner)
    def _():
        arrived = parts_in.at[pl.ds(0, owners - 1)]
        pltpu.make_async_copy(arrived, arrived, c_recv).wait()

    @pl.when(jnp.logical_not(is_owner))
    def _():
        arrived = parts_in.at[pl.ds(0, owners)]
        pltpu.make_async_copy(arrived, arrived, c_recv).wait()

    sum_slots[st] = jnp.sum(parts_in[...].astype(f32), axis=0)

    @pl.loop(1, members)
    def _(step):
        pltpu.make_async_remote_copy(
            src_ref=sum_slots.at[st],
            dst_ref=sum_slots.at[st],
            send_sem=s_send,
            recv_sem=s_recv,
            device_id=(me, lax.rem(st + step, members)),
            device_id_type=MESH,
        ).start()

    others = sum_slots.at[pl.ds(0, members - 1)]
    pltpu.make_async_copy(others, others, s_recv).wait()
    moments = sum_slots[0]
    for member in range(1, members):
        moments = moments + sum_slots[member]

    lane_f = lane_id.astype(f32)
    out_lane = lax.broadcasted_iota(jnp.int32, (cand_count, LANES), 1)
    per_tile = LANES // nodes
    result = jnp.zeros((cand_count, LANES), f32)
    for event in range(events):
        for element in range(elements):
            tile, part = element // per_tile, element % per_tile
            line = moments[tile * events + event : tile * events + event + 1, :]
            mask = lane_f == lane_rows[event] + float(part * nodes)
            value = jnp.sum(jnp.where(mask, line, 0.0), axis=1, keepdims=True)
            result = jnp.where(out_lane == element * events + event, value, result)
    result = jnp.concatenate([result, jnp.zeros((LANES - cand_count, LANES), f32)], axis=0).T
    for element in range(elements):
        rows = result[element * events : (element + 1) * events, :cand_count]
        out_ref[element] = rows

    pltpu.make_async_copy(others, others, s_send).wait()
    sent = gram_slots.at[pl.ds(0, members - 1)]
    pltpu.make_async_copy(sent, sent, gram_send).wait()

    @pl.when(is_owner)
    def _():
        for buffer, sem in ((send_a, a_send), (send_b, b_send), (parts_out, c_send)):
            sent = buffer.at[pl.ds(0, buffer.shape[0] - 1)]
            pltpu.make_async_copy(sent, sent, sem).wait()

    @pl.when(jnp.logical_not(is_owner))
    def _():
        for buffer, sem in ((send_a, a_send), (send_b, b_send)):
            pltpu.make_async_copy(buffer, buffer, sem).wait()


def shards(records, store, taper, candidates, node_slot):
    groups, members = lax.axis_size("ev"), lax.axis_size("st")
    events, stations, comps, samples = records.shape
    elements = store.shape[1]
    traces = stations * comps
    bins = 2 * taper.shape[0]
    owners = traces * bins // (UNITS * LANES)
    cand_count = candidates.shape[1]
    nodes = node_slot.shape[0]
    dims = (groups, members, events, elements, traces, owners, cand_count, nodes)
    units = traces * (bins // LANES)
    f32, bf16 = jnp.float32, jnp.bfloat16
    table = jnp.asarray(band_table(samples, taper.shape[0]))
    rows_a, rows_b = events * UNITS, elements * UNITS
    result = pl.pallas_call(
        functools.partial(kernel, dims),
        out_shape=jax.ShapeDtypeStruct((elements, events, cand_count), f32),
        in_specs=[pl.BlockSpec(memory_space=pltpu.HBM)] * 6,
        out_specs=pl.BlockSpec(memory_space=pltpu.VMEM),
        scratch_shapes=[
            pltpu.VMEM((traces, events, samples), bf16),
            pltpu.VMEM((elements * stations, comps, samples), bf16),
            pltpu.VMEM((samples, bins), bf16),
            pltpu.VMEM((1, taper.shape[0]), f32),
            pltpu.VMEM((events, cand_count), jnp.int32),
            pltpu.VMEM((1, nodes), jnp.int32),
            pltpu.VMEM((elements * traces * (bins // LANES), LANES), f32),
            pltpu.VMEM((events * units, LANES), f32),
            pltpu.VMEM((elements * units, LANES), f32),
            pltpu.VMEM((owners, rows_a, LANES), bf16),
            pltpu.VMEM((owners, rows_b, LANES), bf16),
            pltpu.VMEM((groups, rows_a, LANES), bf16),
            pltpu.VMEM((groups, rows_b, LANES), bf16),
            pltpu.VMEM((groups // CHUNKS * rows_a, LANES), f32),
            pltpu.VMEM((groups * rows_b, LANES), f32),
            pltpu.VMEM((groups // CHUNKS * events, UNITS * LANES), bf16),
            pltpu.VMEM((elements * groups, UNITS * LANES), bf16),
            pltpu.VMEM((groups // CHUNKS * 16, LANES), f32),
            pltpu.VMEM((groups, 16, LANES), bf16),
            pltpu.VMEM((owners, 16, LANES), bf16),
            pltpu.VMEM((members, 24, LANES), f32),
            pltpu.VMEM((members, 16, LANES), f32),
            pltpu.SemaphoreType.DMA((6,)),
        ]
        + [pltpu.SemaphoreType.DMA] * 3
        + [pltpu.SemaphoreType.DMA((CHUNKS,))]
        + [pltpu.SemaphoreType.DMA] * 6,
        compiler_params=pltpu.CompilerParams(
            collective_id=0, has_side_effects=True, vmem_limit_bytes=215 * 256 * 1024
        ),
    )(
        records.transpose(1, 2, 0, 3).reshape(traces, events, samples),
        store.reshape(elements * stations, comps, samples),
        table,
        taper.reshape(1, -1),
        candidates,
        node_slot.reshape(1, -1),
    )
    return result.transpose(1, 2, 0)


def solution(mesh):
    return jax.shard_map(
        shards,
        mesh=mesh,
        in_specs=(
            P("ev", "st", None, None),
            P("ev", None, "st", None, None),
            P(),
            P("ev", None),
            P(),
        ),
        out_specs=P("ev", None, None),
        check_vma=False,
    )
```

```python
import functools
import math

import jax
import jax.numpy as jnp
import numpy as np
from jax import lax
from jax.experimental import pallas as pl
from jax.experimental.pallas import tpu as pltpu
from jax.sharding import PartitionSpec as P

LANES = 128
UNITS = 8
CHUNKS = 4
MESH = pl.DeviceIdType.MESH


def band_table(samples, freq_bins):
    sample_idx = np.arange(samples, dtype=np.int32)[:, None]
    bin_idx = np.arange(1, freq_bins + 1, dtype=np.int32)[None, :]
    phases = sample_idx * bin_idx % samples
    angles = phases.astype(np.float32) * np.float32(2.0 * math.pi / samples)
    table = np.concatenate([np.cos(angles), -np.sin(angles)], axis=1)
    return table.astype(jnp.bfloat16)


def owner_chip(owner, core, owners, groups):
    return ((2 * owner + core) * groups) // (2 * owners)


def around(step, count):
    step = count - 1 - step
    half = (step + 1) // 2
    return jnp.where(lax.rem(step, 2) == 0, half, lax.rem(count - half, count))


def far_rank(offset, count):
    half = count // 2
    return jnp.where(offset < half, 2 * (half - offset) - 1, 2 * (offset - half))


def far_offset(rank, count):
    half = count // 2
    return jnp.where(lax.rem(rank, 2) == 0, half + rank // 2, half - (rank + 1) // 2)


def kernel(
    dims,
    records_hbm,
    store_hbm,
    table_hbm,
    taper_hbm,
    cand_hbm,
    slot_hbm,
    out_ref,
    records_v,
    store_v,
    table_v,
    taper_ref,
    cand_ref,
    slot_ref,
    spectra,
    bands_a,
    bands_b,
    send_a,
    send_b,
    recv_a,
    recv_b,
    wide_a,
    wide_b,
    matrix_a,
    matrix_b,
    mixed,
    parts_out,
    parts_in,
    gram_slots,
    sum_slots,
    load_sem,
    gram_send,
    gram_recv,
    a_send,
    a_recv,
    b_send,
    b_recv,
    c_send,
    c_recv,
    s_send,
    s_recv,
):
    groups, members, events, elements, traces, owners, cand_count, nodes = dims
    me = lax.axis_index("ev")
    st = lax.axis_index("st")
    core = lax.rem(st, 2)
    units = traces * 4
    f32 = jnp.float32
    bf16 = jnp.bfloat16

    loads = [
        pltpu.make_async_copy(table_hbm, table_v, load_sem.at[0]),
        pltpu.make_async_copy(store_hbm, store_v, load_sem.at[1]),
        pltpu.make_async_copy(records_hbm, records_v, load_sem.at[2]),
        pltpu.make_async_copy(taper_hbm, taper_ref, load_sem.at[3]),
        pltpu.make_async_copy(cand_hbm, cand_ref, load_sem.at[4]),
        pltpu.make_async_copy(slot_hbm, slot_ref, load_sem.at[5]),
    ]
    for load in loads:
        load.start()

    barrier = pltpu.get_barrier_semaphore()

    def shifted(index, offset, count):
        total = index + offset
        return jnp.where(total >= count, total - count, total)

    for offset in sorted(range(1, groups), key=lambda at: abs(at - groups // 2)):
        peer = shifted(me, offset, groups)
        pl.semaphore_signal(barrier, inc=1, device_id=(peer, st), device_id_type=MESH)
    far_members = sorted(range(1, members), key=lambda at: abs(at - members // 2))
    for offset in far_members:
        peer = shifted(st, offset, members)
        pl.semaphore_signal(barrier, inc=1, device_id=(me, peer), device_id_type=MESH)

    ranked = (2 * owners * me + groups - 1) // groups
    is_owner = (
        (ranked < 2 * owners)
        & ((ranked * groups) // (2 * owners) == me)
        & (lax.rem(ranked, 2) == core)
    )
    my_owner = ranked // 2
    first = (me * owners) // groups

    loads[0].wait()
    loads[1].wait()
    loads[3].wait()
    height = elements * traces

    def by_tiles(values):
        for tile in range(4):
            start = tile * height
            spectra[start : start + values.shape[0], :] = values[
                :, tile * LANES : (tile + 1) * LANES
            ]

    samples = table_v.shape[0]
    rows = store_v[...].reshape(elements * traces, samples)
    by_tiles(jnp.dot(rows, table_v[...], preferred_element_type=f32))
    for tile in range(4):
        half = (tile % 2) * LANES
        gains = taper_ref[:, half : half + LANES]
        for element in range(elements):
            source = tile * height + element * traces
            block = spectra[source : source + traces, :]
            start = element * units + tile * traces
            bands_b[start : start + traces, :] = (block * gains).astype(bf16).astype(f32)
    pair_at = {}
    for row in range(elements):
        for col in range(row + 1):
            pair_at[row, col] = len(pair_at)
    shares = []
    for (row, col), _ in pair_at.items():
        product = (
            bands_b[row * units : (row + 1) * units, :]
            * bands_b[col * units : (col + 1) * units, :]
        )
        shares.append(jnp.sum(product, axis=0, keepdims=True))
    gram_rows = gram_slots.shape[1]
    shares.append(jnp.zeros((gram_rows - len(shares), LANES), f32))
    gram_slots[st] = jnp.concatenate(shares, axis=0)

    loads[2].wait()
    rows = records_v[...].reshape(traces * events, samples)
    values = rows.astype(f32)
    mean = jnp.sum(values * values, axis=1, keepdims=True) * (1.0 / samples)
    scale = lax.rsqrt(mean + 1e-05) * (1.0 / math.sqrt(samples))
    by_tiles(jnp.dot(rows, table_v[...], preferred_element_type=f32) * scale)
    for tile in range(4):
        for event in range(events):
            block = spectra[pl.ds(tile * height + event, traces, stride=events), :]
            start = event * units + tile * traces
            bands_a[start : start + traces, :] = block

    def rows_of(index, owner):
        return pl.ds(pl.multiple_of(index * units + owner * UNITS, UNITS), UNITS)

    @pl.loop(0, owners)
    def _(owner):
        for pair in range(events // 2):
            tile = jnp.concatenate(
                [bands_a[rows_of(2 * pair, owner), :], bands_a[rows_of(2 * pair + 1, owner), :]],
                axis=0,
            )
            send_a[owner, 2 * UNITS * pair : 2 * UNITS * (pair + 1), :] = tile.astype(bf16)

    pl.semaphore_wait(barrier, groups + members - 2)

    def gram_copy(step):
        return pltpu.make_async_remote_copy(
            src_ref=gram_slots.at[st],
            dst_ref=gram_slots.at[st],
            send_sem=gram_send,
            recv_sem=gram_recv,
            device_id=(me, shifted(st, step, members)),
            device_id_type=MESH,
        )

    for step in far_members:
        gram_copy(step).start()

    def send_block(buffer, slots, owner, slot, send_sem, recv_sem):
        chip = owner_chip(owner, core, owners, groups)

        @pl.when(chip != me)
        def _():
            pltpu.make_async_remote_copy(
                src_ref=buffer.at[owner],
                dst_ref=slots.at[slot],
                send_sem=send_sem,
                recv_sem=recv_sem,
                device_id=(chip, st),
                device_id_type=MESH,
            ).start()

        @pl.when(chip == me)
        def _():
            slots[slot] = buffer[owner]

    span = groups // CHUNKS

    def send_observed(step):
        owner = lax.rem(first + around(step, owners), owners)
        offset = lax.rem(owner_chip(owner, core, owners, groups) - me + groups, groups)
        rank = far_rank(offset, groups)
        send_block(send_a, recv_a, owner, rank, a_send, a_recv.at[rank // span])

    early = owners // 2

    @pl.loop(0, early)
    def _(step):
        send_observed(step)

    others = gram_slots.at[pl.ds(0, members - 1)]
    pltpu.make_async_copy(others, others, gram_recv).wait()
    total = gram_slots[0]
    for member in range(1, members):
        total = total + gram_slots[member]
    total = jnp.broadcast_to(jnp.sum(total, axis=1, keepdims=True), total.shape)
    factor = {}
    inverse = []
    for row in range(elements):
        for col in range(row + 1):
            at = pair_at[row, col]
            running = total[at : at + 1, :]
            for mid in range(col):
                running = running - factor[row, mid] * factor[col, mid]
            if row == col:
                root = jnp.sqrt(running)
                inverse.append(1.0 / root)
            else:
                factor[row, col] = running * inverse[col]
    factor = {at: jnp.broadcast_to(value, (UNITS, LANES)) for at, value in factor.items()}
    inverse = [jnp.broadcast_to(value, (UNITS, LANES)) for value in inverse]

    @pl.loop(0, owners)
    def _(step):
        owner = lax.rem(first + around(step, owners), owners)
        forward = []
        for row in range(elements):
            running = bands_b[rows_of(row, owner), :]
            for mid in range(row):
                running = running - factor[row, mid] * forward[mid]
            forward.append(running * inverse[row])
        answer = [None] * elements
        for row in reversed(range(elements)):
            running = forward[row]
            for mid in range(row + 1, elements):
                running = running - factor[mid, row] * answer[mid]
            answer[row] = running * inverse[row]
        for pair in range(elements // 2):
            tile = jnp.concatenate([answer[2 * pair], answer[2 * pair + 1]], axis=0)
            send_b[owner, 2 * UNITS * pair : 2 * UNITS * (pair + 1), :] = tile.astype(bf16)
        send_block(send_b, recv_b, owner, me, b_send, b_recv)

    @pl.loop(early, owners)
    def _(step):
        send_observed(step)

    loads[4].wait()
    loads[5].wait()
    lane_id = lax.broadcasted_iota(jnp.int32, (cand_count, LANES), 1)
    node_id = lax.broadcasted_iota(jnp.int32, (cand_count, nodes), 1)
    eye = lax.broadcasted_iota(jnp.int32, (cand_count, cand_count), 0) == (
        lax.broadcasted_iota(jnp.int32, (cand_count, cand_count), 1)
    )
    slot_values = slot_ref[...].astype(f32)
    lane_rows = []
    for event in range(events):
        wanted = jnp.where(eye, cand_ref[event : event + 1, :].astype(f32), 0.0)
        wanted = jnp.sum(wanted, axis=1, keepdims=True)
        chosen = jnp.where(node_id.astype(f32) == wanted, slot_values, 0.0)
        lane_rows.append(jnp.sum(chosen, axis=1, keepdims=True))

    def spread(wide, target, count, height):
        @pl.loop(0, UNITS)
        def _(unit):
            lanes = pl.ds(pl.multiple_of(unit * LANES, LANES), LANES)
            for row in range(count):
                picked = wide[pl.ds(row * UNITS + unit, height, stride=count * UNITS), :]
                target[row * height : (row + 1) * height, lanes] = picked.astype(bf16)

    @pl.when(is_owner)
    def _():
        mixed[...] = jnp.zeros_like(mixed)
        arrived = recv_b.at[pl.ds(0, groups - 1)]
        pltpu.make_async_copy(arrived, arrived, b_recv).wait()
        wide_b[...] = recv_b[...].astype(f32).reshape(wide_b.shape)
        spread(wide_b, matrix_b, elements, groups)
        for chunk in range(CHUNKS):
            start, stop = chunk * span, (chunk + 1) * span
            remote = min(stop, groups - 1)
            arrived = recv_a.at[pl.ds(start, remote - start)]
            pltpu.make_async_copy(arrived, arrived, a_recv.at[chunk]).wait()
            wide_a[...] = recv_a[start:stop].astype(f32).reshape(wide_a.shape)
            spread(wide_a, matrix_a, events, span)
            products = lax.dot_general(
                matrix_a[...],
                matrix_b[...],
                (((1,), (1,)), ((), ())),
                preferred_element_type=f32,
            )
            for tile in range(elements * nodes // LANES):
                for event in range(events):
                    mixed[pl.ds(tile * events + event, span, stride=16), :] = products[
                        event * span : (event + 1) * span, tile * LANES : (tile + 1) * LANES
                    ]
            parts_out[start:stop] = mixed[...].astype(bf16).reshape(span, 16, LANES)

            @pl.loop(start, remote)
            def _(rank):
                peer = lax.rem(me - far_offset(rank, groups) + groups, groups)
                pltpu.make_async_remote_copy(
                    src_ref=parts_out.at[rank],
                    dst_ref=parts_in.at[my_owner],
                    send_sem=c_send,
                    recv_sem=c_recv,
                    device_id=(peer, st),
                    device_id_type=MESH,
                ).start()

        parts_in[my_owner] = parts_out[groups - 1]

    @pl.when(is_owner)
    def _():
        arrived = parts_in.at[pl.ds(0, owners - 1)]
        pltpu.make_async_copy(arrived, arrived, c_recv).wait()

    @pl.when(jnp.logical_not(is_owner))
    def _():
        arrived = parts_in.at[pl.ds(0, owners)]
        pltpu.make_async_copy(arrived, arrived, c_recv).wait()

    sum_slots[st] = jnp.sum(parts_in[...].astype(f32), axis=0)

    for step in far_members:
        pltpu.make_async_remote_copy(
            src_ref=sum_slots.at[st],
            dst_ref=sum_slots.at[st],
            send_sem=s_send,
            recv_sem=s_recv,
            device_id=(me, shifted(st, step, members)),
            device_id_type=MESH,
        ).start()

    others = sum_slots.at[pl.ds(0, members - 1)]
    pltpu.make_async_copy(others, others, s_recv).wait()
    moments = sum_slots[0]
    for member in range(1, members):
        moments = moments + sum_slots[member]

    lane_f = lane_id.astype(f32)
    out_lane = lax.broadcasted_iota(jnp.int32, (cand_count, LANES), 1)
    per_tile = LANES // nodes
    result = jnp.zeros((cand_count, LANES), f32)
    for event in range(events):
        for element in range(elements):
            tile, part = element // per_tile, element % per_tile
            line = moments[tile * events + event : tile * events + event + 1, :]
            mask = lane_f == lane_rows[event] + float(part * nodes)
            value = jnp.sum(jnp.where(mask, line, 0.0), axis=1, keepdims=True)
            result = jnp.where(out_lane == element * events + event, value, result)
    result = jnp.concatenate([result, jnp.zeros((LANES - cand_count, LANES), f32)], axis=0).T
    for element in range(elements):
        rows = result[element * events : (element + 1) * events, :cand_count]
        out_ref[element] = rows

    pltpu.make_async_copy(others, others, s_send).wait()
    sent = gram_slots.at[pl.ds(0, members - 1)]
    pltpu.make_async_copy(sent, sent, gram_send).wait()

    @pl.when(is_owner)
    def _():
        for buffer, sem in ((send_a, a_send), (send_b, b_send), (parts_out, c_send)):
            sent = buffer.at[pl.ds(0, buffer.shape[0] - 1)]
            pltpu.make_async_copy(sent, sent, sem).wait()

    @pl.when(jnp.logical_not(is_owner))
    def _():
        for buffer, sem in ((send_a, a_send), (send_b, b_send)):
            pltpu.make_async_copy(buffer, buffer, sem).wait()


def shards(records, store, taper, candidates, node_slot):
    groups, members = lax.axis_size("ev"), lax.axis_size("st")
    events, stations, comps, samples = records.shape
    elements = store.shape[1]
    traces = stations * comps
    bins = 2 * taper.shape[0]
    owners = traces * bins // (UNITS * LANES)
    cand_count = candidates.shape[1]
    nodes = node_slot.shape[0]
    dims = (groups, members, events, elements, traces, owners, cand_count, nodes)
    units = traces * (bins // LANES)
    f32, bf16 = jnp.float32, jnp.bfloat16
    table = jnp.asarray(band_table(samples, taper.shape[0]))
    rows_a, rows_b = events * UNITS, elements * UNITS
    result = pl.pallas_call(
        functools.partial(kernel, dims),
        out_shape=jax.ShapeDtypeStruct((elements, events, cand_count), f32),
        in_specs=[pl.BlockSpec(memory_space=pltpu.HBM)] * 6,
        out_specs=pl.BlockSpec(memory_space=pltpu.VMEM),
        scratch_shapes=[
            pltpu.VMEM((traces, events, samples), bf16),
            pltpu.VMEM((elements * stations, comps, samples), bf16),
            pltpu.VMEM((samples, bins), bf16),
            pltpu.VMEM((1, taper.shape[0]), f32),
            pltpu.VMEM((events, cand_count), jnp.int32),
            pltpu.VMEM((1, nodes), jnp.int32),
            pltpu.VMEM((elements * traces * (bins // LANES), LANES), f32),
            pltpu.VMEM((events * units, LANES), f32),
            pltpu.VMEM((elements * units, LANES), f32),
            pltpu.VMEM((owners, rows_a, LANES), bf16),
            pltpu.VMEM((owners, rows_b, LANES), bf16),
            pltpu.VMEM((groups, rows_a, LANES), bf16),
            pltpu.VMEM((groups, rows_b, LANES), bf16),
            pltpu.VMEM((groups // CHUNKS * rows_a, LANES), f32),
            pltpu.VMEM((groups * rows_b, LANES), f32),
            pltpu.VMEM((groups // CHUNKS * events, UNITS * LANES), bf16),
            pltpu.VMEM((elements * groups, UNITS * LANES), bf16),
            pltpu.VMEM((groups // CHUNKS * 16, LANES), f32),
            pltpu.VMEM((groups, 16, LANES), bf16),
            pltpu.VMEM((owners, 16, LANES), bf16),
            pltpu.VMEM((members, 24, LANES), f32),
            pltpu.VMEM((members, 16, LANES), f32),
            pltpu.SemaphoreType.DMA((6,)),
        ]
        + [pltpu.SemaphoreType.DMA] * 3
        + [pltpu.SemaphoreType.DMA((CHUNKS,))]
        + [pltpu.SemaphoreType.DMA] * 6,
        compiler_params=pltpu.CompilerParams(
            collective_id=0, has_side_effects=True, vmem_limit_bytes=215 * 256 * 1024
        ),
    )(
        records.transpose(1, 2, 0, 3).reshape(traces, events, samples),
        store.reshape(elements * stations, comps, samples),
        table,
        taper.reshape(1, -1),
        candidates,
        node_slot.reshape(1, -1),
    )
    return result.transpose(1, 2, 0)


def solution(mesh):
    return jax.shard_map(
        shards,
        mesh=mesh,
        in_specs=(
            P("ev", "st", None, None),
            P("ev", None, "st", None, None),
            P(),
            P("ev", None),
            P(),
        ),
        out_specs=P("ev", None, None),
        check_vma=False,
    )
```

```python
import functools
import math

import jax
import jax.numpy as jnp
import numpy as np
from jax import lax
from jax.experimental import pallas as pl
from jax.experimental.pallas import tpu as pltpu
from jax.sharding import PartitionSpec as P

LANES = 128
UNITS = 8
CHUNKS = 4
MESH = pl.DeviceIdType.MESH


def band_table(samples, freq_bins):
    sample_idx = np.arange(samples, dtype=np.int32)[:, None]
    bin_idx = np.arange(1, freq_bins + 1, dtype=np.int32)[None, :]
    phases = sample_idx * bin_idx % samples
    angles = phases.astype(np.float32) * np.float32(2.0 * math.pi / samples)
    table = np.concatenate([np.cos(angles), -np.sin(angles)], axis=1)
    return table.astype(jnp.bfloat16)


def owner_chip(owner, core, owners, groups):
    return ((2 * owner + core) * groups) // (2 * owners)


def around(step, count):
    step = count - 1 - step
    half = (step + 1) // 2
    return jnp.where(lax.rem(step, 2) == 0, half, lax.rem(count - half, count))


def far_rank(offset, count):
    half = count // 2
    return jnp.where(offset < half, 2 * (half - offset) - 1, 2 * (offset - half))


def far_offset(rank, count):
    half = count // 2
    return jnp.where(lax.rem(rank, 2) == 0, half + rank // 2, half - (rank + 1) // 2)


def kernel(
    dims,
    records_hbm,
    store_hbm,
    table_hbm,
    taper_hbm,
    cand_hbm,
    slot_hbm,
    out_ref,
    records_v,
    store_v,
    table_v,
    taper_ref,
    cand_ref,
    slot_ref,
    spectra,
    bands_a,
    bands_b,
    send_a,
    send_b,
    recv_a,
    recv_b,
    wide_a,
    wide_b,
    matrix_a,
    matrix_b,
    mixed,
    parts_out,
    parts_in,
    gram_slots,
    sum_slots,
    load_sem,
    gram_send,
    gram_recv,
    a_send,
    a_recv,
    b_send,
    b_recv,
    c_send,
    c_recv,
    s_send,
    s_recv,
):
    groups, members, events, elements, traces, owners, cand_count, nodes = dims
    me = lax.axis_index("ev")
    st = lax.axis_index("st")
    core = lax.rem(st, 2)
    units = traces * 4
    f32 = jnp.float32
    bf16 = jnp.bfloat16

    loads = [
        pltpu.make_async_copy(table_hbm, table_v, load_sem.at[0]),
        pltpu.make_async_copy(store_hbm, store_v, load_sem.at[1]),
        pltpu.make_async_copy(records_hbm, records_v, load_sem.at[2]),
        pltpu.make_async_copy(taper_hbm, taper_ref, load_sem.at[3]),
        pltpu.make_async_copy(cand_hbm, cand_ref, load_sem.at[4]),
        pltpu.make_async_copy(slot_hbm, slot_ref, load_sem.at[5]),
    ]
    for load in loads:
        load.start()

    barrier = pltpu.get_barrier_semaphore()

    def shifted(index, offset, count):
        total = index + offset
        return jnp.where(total >= count, total - count, total)

    for offset in sorted(range(1, groups), key=lambda at: abs(at - groups // 2)):
        peer = shifted(me, offset, groups)
        pl.semaphore_signal(barrier, inc=1, device_id=(peer, st), device_id_type=MESH)
    far_members = sorted(range(1, members), key=lambda at: abs(at - members // 2))
    for offset in far_members:
        peer = shifted(st, offset, members)
        pl.semaphore_signal(barrier, inc=1, device_id=(me, peer), device_id_type=MESH)

    ranked = (2 * owners * me + groups - 1) // groups
    is_owner = (
        (ranked < 2 * owners)
        & ((ranked * groups) // (2 * owners) == me)
        & (lax.rem(ranked, 2) == core)
    )
    my_owner = ranked // 2
    first = (me * owners) // groups

    loads[0].wait()
    loads[1].wait()
    loads[3].wait()
    height = elements * traces

    def by_tiles(values):
        for tile in range(4):
            start = tile * height
            spectra[start : start + values.shape[0], :] = values[
                :, tile * LANES : (tile + 1) * LANES
            ]

    samples = table_v.shape[0]
    rows = store_v[...].reshape(elements * traces, samples)
    by_tiles(jnp.dot(rows, table_v[...], preferred_element_type=f32))
    for tile in range(4):
        half = (tile % 2) * LANES
        gains = taper_ref[:, half : half + LANES]
        for element in range(elements):
            source = tile * height + element * traces
            block = spectra[source : source + traces, :]
            start = element * units + tile * traces
            bands_b[start : start + traces, :] = (block * gains).astype(bf16).astype(f32)
    pair_at = {}
    for row in range(elements):
        for col in range(row + 1):
            pair_at[row, col] = len(pair_at)
    shares = []
    for (row, col), _ in pair_at.items():
        product = (
            bands_b[row * units : (row + 1) * units, :]
            * bands_b[col * units : (col + 1) * units, :]
        )
        shares.append(jnp.sum(product, axis=0, keepdims=True))
    gram_rows = gram_slots.shape[1]
    shares.append(jnp.zeros((gram_rows - len(shares), LANES), f32))
    gram_slots[st] = jnp.concatenate(shares, axis=0)

    loads[2].wait()
    rows = records_v[...].reshape(traces * events, samples)
    values = rows.astype(f32)
    mean = jnp.sum(values * values, axis=1, keepdims=True) * (1.0 / samples)
    scale = lax.rsqrt(mean + 1e-05) * (1.0 / math.sqrt(samples))
    by_tiles(jnp.dot(rows, table_v[...], preferred_element_type=f32) * scale)
    for tile in range(4):
        for event in range(events):
            block = spectra[pl.ds(tile * height + event, traces, stride=events), :]
            start = event * units + tile * traces
            bands_a[start : start + traces, :] = block

    def rows_of(index, owner):
        return pl.ds(pl.multiple_of(index * units + owner * UNITS, UNITS), UNITS)

    @pl.loop(0, owners)
    def _(owner):
        for pair in range(events // 2):
            tile = jnp.concatenate(
                [bands_a[rows_of(2 * pair, owner), :], bands_a[rows_of(2 * pair + 1, owner), :]],
                axis=0,
            )
            send_a[owner, 2 * UNITS * pair : 2 * UNITS * (pair + 1), :] = tile.astype(bf16)

    pl.semaphore_wait(barrier, groups + members - 2)

    def gram_copy(step):
        return pltpu.make_async_remote_copy(
            src_ref=gram_slots.at[st],
            dst_ref=gram_slots.at[st],
            send_sem=gram_send,
            recv_sem=gram_recv,
            device_id=(me, shifted(st, step, members)),
            device_id_type=MESH,
        )

    for step in far_members:
        gram_copy(step).start()

    def send_block(buffer, slots, owner, slot, send_sem, recv_sem):
        chip = owner_chip(owner, core, owners, groups)

        @pl.when(chip != me)
        def _():
            pltpu.make_async_remote_copy(
                src_ref=buffer.at[owner],
                dst_ref=slots.at[slot],
                send_sem=send_sem,
                recv_sem=recv_sem,
                device_id=(chip, st),
                device_id_type=MESH,
            ).start()

        @pl.when(chip == me)
        def _():
            slots[slot] = buffer[owner]

    span = groups // CHUNKS

    def send_observed(step):
        owner = lax.rem(first + around(step, owners), owners)
        offset = lax.rem(owner_chip(owner, core, owners, groups) - me + groups, groups)
        rank = far_rank(offset, groups)
        send_block(send_a, recv_a, owner, rank, a_send, a_recv.at[rank // span])

    early = owners // 2

    @pl.loop(0, early)
    def _(step):
        send_observed(step)

    others = gram_slots.at[pl.ds(0, members - 1)]
    pltpu.make_async_copy(others, others, gram_recv).wait()
    total = gram_slots[0]
    for member in range(1, members):
        total = total + gram_slots[member]
    total = jnp.broadcast_to(jnp.sum(total, axis=1, keepdims=True), total.shape)
    factor = {}
    inverse = []
    for row in range(elements):
        for col in range(row + 1):
            at = pair_at[row, col]
            running = total[at : at + 1, :]
            for mid in range(col):
                running = running - factor[row, mid] * factor[col, mid]
            if row == col:
                root = jnp.sqrt(running)
                inverse.append(1.0 / root)
            else:
                factor[row, col] = running * inverse[col]
    factor = {at: jnp.broadcast_to(value, (UNITS, LANES)) for at, value in factor.items()}
    inverse = [jnp.broadcast_to(value, (UNITS, LANES)) for value in inverse]

    @pl.loop(0, owners)
    def _(step):
        owner = lax.rem(first + around(step, owners), owners)
        forward = []
        for row in range(elements):
            running = bands_b[rows_of(row, owner), :]
            for mid in range(row):
                running = running - factor[row, mid] * forward[mid]
            forward.append(running * inverse[row])
        answer = [None] * elements
        for row in reversed(range(elements)):
            running = forward[row]
            for mid in range(row + 1, elements):
                running = running - factor[mid, row] * answer[mid]
            answer[row] = running * inverse[row]
        for pair in range(elements // 2):
            tile = jnp.concatenate([answer[2 * pair], answer[2 * pair + 1]], axis=0)
            send_b[owner, 2 * UNITS * pair : 2 * UNITS * (pair + 1), :] = tile.astype(bf16)
        send_block(send_b, recv_b, owner, me, b_send, b_recv)

    @pl.loop(early, owners)
    def _(step):
        send_observed(step)

    loads[4].wait()
    loads[5].wait()
    lane_id = lax.broadcasted_iota(jnp.int32, (cand_count, LANES), 1)
    node_id = lax.broadcasted_iota(jnp.int32, (cand_count, nodes), 1)
    eye = lax.broadcasted_iota(jnp.int32, (cand_count, cand_count), 0) == (
        lax.broadcasted_iota(jnp.int32, (cand_count, cand_count), 1)
    )
    slot_values = slot_ref[...].astype(f32)
    lane_rows = []
    for event in range(events):
        wanted = jnp.where(eye, cand_ref[event : event + 1, :].astype(f32), 0.0)
        wanted = jnp.sum(wanted, axis=1, keepdims=True)
        chosen = jnp.where(node_id.astype(f32) == wanted, slot_values, 0.0)
        lane_rows.append(jnp.sum(chosen, axis=1, keepdims=True))

    def spread(wide, target, count, height):
        @pl.loop(0, UNITS)
        def _(unit):
            lanes = pl.ds(pl.multiple_of(unit * LANES, LANES), LANES)
            for row in range(count):
                picked = wide[pl.ds(row * UNITS + unit, height, stride=count * UNITS), :]
                target[row * height : (row + 1) * height, lanes] = picked.astype(bf16)

    @pl.when(is_owner)
    def _():
        mixed[...] = jnp.zeros_like(mixed)
        arrived = recv_b.at[pl.ds(0, groups - 1)]
        pltpu.make_async_copy(arrived, arrived, b_recv).wait()
        wide_b[0 : groups * elements * UNITS, :] = (
            recv_b[...].astype(f32).reshape(groups * elements * UNITS, LANES)
        )
        spread(wide_b, matrix_b, elements, groups)
        for chunk in range(CHUNKS):
            start, stop = chunk * span, (chunk + 1) * span
            remote = min(stop, groups - 1)
            arrived = recv_a.at[pl.ds(start, remote - start)]
            pltpu.make_async_copy(arrived, arrived, a_recv.at[chunk]).wait()
            wide_a[0 : span * events * UNITS, :] = (
                recv_a[start:stop].astype(f32).reshape(span * events * UNITS, LANES)
            )
            spread(wide_a, matrix_a, events, span)
            products = lax.dot_general(
                matrix_a[...],
                matrix_b[...],
                (((1,), (1,)), ((), ())),
                preferred_element_type=f32,
            )
            for tile in range(elements * nodes // LANES):
                for event in range(events):
                    mixed[pl.ds(tile * events + event, span, stride=16), :] = products[
                        event * span : (event + 1) * span, tile * LANES : (tile + 1) * LANES
                    ]
            parts_out[start:stop] = (
                mixed[0 : span * 16, :].astype(bf16).reshape(span, 16, LANES)
            )

            @pl.loop(start, remote)
            def _(rank):
                peer = lax.rem(me - far_offset(rank, groups) + groups, groups)
                pltpu.make_async_remote_copy(
                    src_ref=parts_out.at[rank],
                    dst_ref=parts_in.at[my_owner],
                    send_sem=c_send,
                    recv_sem=c_recv,
                    device_id=(peer, st),
                    device_id_type=MESH,
                ).start()

        parts_in[my_owner] = parts_out[groups - 1]

    @pl.when(is_owner)
    def _():
        arrived = parts_in.at[pl.ds(0, owners - 1)]
        pltpu.make_async_copy(arrived, arrived, c_recv).wait()

    @pl.when(jnp.logical_not(is_owner))
    def _():
        arrived = parts_in.at[pl.ds(0, owners)]
        pltpu.make_async_copy(arrived, arrived, c_recv).wait()

    sum_slots[st] = jnp.sum(parts_in[...].astype(f32), axis=0)

    for step in far_members:
        pltpu.make_async_remote_copy(
            src_ref=sum_slots.at[st],
            dst_ref=sum_slots.at[st],
            send_sem=s_send,
            recv_sem=s_recv,
            device_id=(me, shifted(st, step, members)),
            device_id_type=MESH,
        ).start()

    others = sum_slots.at[pl.ds(0, members - 1)]
    pltpu.make_async_copy(others, others, s_recv).wait()
    moments = sum_slots[0]
    for member in range(1, members):
        moments = moments + sum_slots[member]

    lane_f = lane_id.astype(f32)
    out_lane = lax.broadcasted_iota(jnp.int32, (cand_count, LANES), 1)
    per_tile = LANES // nodes
    result = jnp.zeros((cand_count, LANES), f32)
    for event in range(events):
        for element in range(elements):
            tile, part = element // per_tile, element % per_tile
            line = moments[tile * events + event : tile * events + event + 1, :]
            mask = lane_f == lane_rows[event] + float(part * nodes)
            value = jnp.sum(jnp.where(mask, line, 0.0), axis=1, keepdims=True)
            result = jnp.where(out_lane == element * events + event, value, result)
    result = jnp.concatenate([result, jnp.zeros((LANES - cand_count, LANES), f32)], axis=0).T
    for element in range(elements):
        rows = result[element * events : (element + 1) * events, :cand_count]
        out_ref[element] = rows

    pltpu.make_async_copy(others, others, s_send).wait()
    sent = gram_slots.at[pl.ds(0, members - 1)]
    pltpu.make_async_copy(sent, sent, gram_send).wait()

    @pl.when(is_owner)
    def _():
        for buffer, sem in ((send_a, a_send), (send_b, b_send), (parts_out, c_send)):
            sent = buffer.at[pl.ds(0, buffer.shape[0] - 1)]
            pltpu.make_async_copy(sent, sent, sem).wait()

    @pl.when(jnp.logical_not(is_owner))
    def _():
        for buffer, sem in ((send_a, a_send), (send_b, b_send)):
            pltpu.make_async_copy(buffer, buffer, sem).wait()


def shards(records, store, taper, candidates, node_slot):
    groups, members = lax.axis_size("ev"), lax.axis_size("st")
    events, stations, comps, samples = records.shape
    elements = store.shape[1]
    traces = stations * comps
    bins = 2 * taper.shape[0]
    owners = traces * bins // (UNITS * LANES)
    cand_count = candidates.shape[1]
    nodes = node_slot.shape[0]
    dims = (groups, members, events, elements, traces, owners, cand_count, nodes)
    units = traces * (bins // LANES)
    f32, bf16 = jnp.float32, jnp.bfloat16
    table = jnp.asarray(band_table(samples, taper.shape[0]))
    rows_a, rows_b = events * UNITS, elements * UNITS
    result = pl.pallas_call(
        functools.partial(kernel, dims),
        out_shape=jax.ShapeDtypeStruct((elements, events, cand_count), f32),
        in_specs=[pl.BlockSpec(memory_space=pltpu.HBM)] * 6,
        out_specs=pl.BlockSpec(memory_space=pltpu.VMEM),
        scratch_shapes=[
            pltpu.VMEM((traces, events, samples), bf16),
            pltpu.VMEM((elements * stations, comps, samples), bf16),
            pltpu.VMEM((samples, bins), bf16),
            pltpu.VMEM((1, taper.shape[0]), f32),
            pltpu.VMEM((events, cand_count), jnp.int32),
            pltpu.VMEM((1, nodes), jnp.int32),
            pltpu.VMEM((elements * traces * (bins // LANES), LANES), f32),
            pltpu.VMEM((events * units, LANES), f32),
            pltpu.VMEM((elements * units, LANES), f32),
            pltpu.VMEM((owners, rows_a, LANES), bf16),
            pltpu.VMEM((owners, rows_b, LANES), bf16),
            pltpu.VMEM((groups, rows_a, LANES), bf16),
            pltpu.VMEM((groups, rows_b, LANES), bf16),
            pltpu.VMEM(((groups // CHUNKS + 1) * rows_a, LANES), f32),
            pltpu.VMEM(((groups + 1) * rows_b, LANES), f32),
            pltpu.VMEM((groups // CHUNKS * events, UNITS * LANES), bf16),
            pltpu.VMEM((elements * groups, UNITS * LANES), bf16),
            pltpu.VMEM(((groups // CHUNKS + 1) * 16, LANES), f32),
            pltpu.VMEM((groups, 16, LANES), bf16),
            pltpu.VMEM((owners, 16, LANES), bf16),
            pltpu.VMEM((members, 24, LANES), f32),
            pltpu.VMEM((members, 16, LANES), f32),
            pltpu.SemaphoreType.DMA((6,)),
        ]
        + [pltpu.SemaphoreType.DMA] * 3
        + [pltpu.SemaphoreType.DMA((CHUNKS,))]
        + [pltpu.SemaphoreType.DMA] * 6,
        compiler_params=pltpu.CompilerParams(
            collective_id=0, has_side_effects=True, vmem_limit_bytes=215 * 256 * 1024
        ),
    )(
        records.transpose(1, 2, 0, 3).reshape(traces, events, samples),
        store.reshape(elements * stations, comps, samples),
        table,
        taper.reshape(1, -1),
        candidates,
        node_slot.reshape(1, -1),
    )
    return result.transpose(1, 2, 0)


def solution(mesh):
    return jax.shard_map(
        shards,
        mesh=mesh,
        in_specs=(
            P("ev", "st", None, None),
            P("ev", None, "st", None, None),
            P(),
            P("ev", None),
            P(),
        ),
        out_specs=P("ev", None, None),
        check_vma=False,
    )
```

```python
import functools
import math

import jax
import jax.numpy as jnp
import numpy as np
from jax import lax
from jax.experimental import pallas as pl
from jax.experimental.pallas import tpu as pltpu
from jax.sharding import PartitionSpec as P

LANES = 128
UNITS = 8
CHUNKS = 4
MESH = pl.DeviceIdType.MESH


def band_table(samples, freq_bins):
    sample_idx = np.arange(samples, dtype=np.int32)[:, None]
    bin_idx = np.arange(1, freq_bins + 1, dtype=np.int32)[None, :]
    phases = sample_idx * bin_idx % samples
    angles = phases.astype(np.float32) * np.float32(2.0 * math.pi / samples)
    table = np.concatenate([np.cos(angles), -np.sin(angles)], axis=1)
    return table.astype(jnp.bfloat16)


def owner_chip(owner, core, owners, groups):
    return ((2 * owner + core) * groups) // (2 * owners)


def around(step, count):
    step = count - 1 - step
    half = (step + 1) // 2
    return jnp.where(lax.rem(step, 2) == 0, half, lax.rem(count - half, count))


def far_rank(offset, count):
    half = count // 2
    return jnp.where(offset < half, 2 * (half - offset) - 1, 2 * (offset - half))


def far_offset(rank, count):
    half = count // 2
    return jnp.where(lax.rem(rank, 2) == 0, half + rank // 2, half - (rank + 1) // 2)


def kernel(
    dims,
    records_hbm,
    store_hbm,
    table_hbm,
    taper_hbm,
    cand_hbm,
    slot_hbm,
    out_ref,
    records_v,
    store_v,
    table_v,
    taper_ref,
    cand_ref,
    slot_ref,
    spectra,
    bands_a,
    bands_b,
    send_a,
    send_b,
    recv_a,
    recv_b,
    wide_a,
    wide_b,
    matrix_a,
    matrix_b,
    mixed,
    parts_out,
    parts_in,
    gram_slots,
    sum_slots,
    load_sem,
    gram_send,
    gram_recv,
    a_send,
    a_recv,
    b_send,
    b_recv,
    c_send,
    c_recv,
    s_send,
    s_recv,
):
    groups, members, events, elements, traces, owners, cand_count, nodes = dims
    me = lax.axis_index("ev")
    st = lax.axis_index("st")
    core = lax.rem(st, 2)
    units = traces * 4
    f32 = jnp.float32
    bf16 = jnp.bfloat16

    loads = [
        pltpu.make_async_copy(table_hbm, table_v, load_sem.at[0]),
        pltpu.make_async_copy(store_hbm, store_v, load_sem.at[1]),
        pltpu.make_async_copy(records_hbm, records_v, load_sem.at[2]),
        pltpu.make_async_copy(taper_hbm, taper_ref, load_sem.at[3]),
        pltpu.make_async_copy(cand_hbm, cand_ref, load_sem.at[4]),
        pltpu.make_async_copy(slot_hbm, slot_ref, load_sem.at[5]),
    ]
    for load in loads:
        load.start()

    barrier = pltpu.get_barrier_semaphore()

    def shifted(index, offset, count):
        total = index + offset
        return jnp.where(total >= count, total - count, total)

    for offset in sorted(range(1, groups), key=lambda at: abs(at - groups // 2)):
        peer = shifted(me, offset, groups)
        pl.semaphore_signal(barrier, inc=1, device_id=(peer, st), device_id_type=MESH)
    far_members = sorted(range(1, members), key=lambda at: abs(at - members // 2))
    for offset in far_members:
        peer = shifted(st, offset, members)
        pl.semaphore_signal(barrier, inc=1, device_id=(me, peer), device_id_type=MESH)

    ranked = (2 * owners * me + groups - 1) // groups
    is_owner = (
        (ranked < 2 * owners)
        & ((ranked * groups) // (2 * owners) == me)
        & (lax.rem(ranked, 2) == core)
    )
    my_owner = ranked // 2
    first = (me * owners) // groups

    loads[0].wait()
    loads[1].wait()
    loads[3].wait()
    height = elements * traces

    def by_tiles(values):
        for tile in range(4):
            start = tile * height
            spectra[start : start + values.shape[0], :] = values[
                :, tile * LANES : (tile + 1) * LANES
            ]

    samples = table_v.shape[0]
    rows = store_v[...].reshape(elements * traces, samples)
    by_tiles(jnp.dot(rows, table_v[...], preferred_element_type=f32))
    for tile in range(4):
        half = (tile % 2) * LANES
        gains = taper_ref[:, half : half + LANES]
        for element in range(elements):
            source = tile * height + element * traces
            block = spectra[source : source + traces, :]
            start = element * units + tile * traces
            bands_b[start : start + traces, :] = (block * gains).astype(bf16).astype(f32)
    pair_at = {}
    for row in range(elements):
        for col in range(row + 1):
            pair_at[row, col] = len(pair_at)
    shares = []
    for (row, col), _ in pair_at.items():
        product = (
            bands_b[row * units : (row + 1) * units, :]
            * bands_b[col * units : (col + 1) * units, :]
        )
        shares.append(jnp.sum(product, axis=0, keepdims=True))
    gram_rows = gram_slots.shape[1]
    shares.append(jnp.zeros((gram_rows - len(shares), LANES), f32))
    gram_slots[st] = jnp.concatenate(shares, axis=0)

    loads[2].wait()
    rows = records_v[...].reshape(traces * events, samples)
    values = rows.astype(f32)
    mean = jnp.sum(values * values, axis=1, keepdims=True) * (1.0 / samples)
    scale = lax.rsqrt(mean + 1e-05) * (1.0 / math.sqrt(samples))
    by_tiles(jnp.dot(rows, table_v[...], preferred_element_type=f32) * scale)
    for tile in range(4):
        for event in range(events):
            block = spectra[pl.ds(tile * height + event, traces, stride=events), :]
            start = event * units + tile * traces
            bands_a[start : start + traces, :] = block

    def rows_of(index, owner):
        return pl.ds(pl.multiple_of(index * units + owner * UNITS, UNITS), UNITS)

    @pl.loop(0, owners)
    def _(owner):
        for pair in range(events // 2):
            tile = jnp.concatenate(
                [bands_a[rows_of(2 * pair, owner), :], bands_a[rows_of(2 * pair + 1, owner), :]],
                axis=0,
            )
            send_a[owner, 2 * UNITS * pair : 2 * UNITS * (pair + 1), :] = tile.astype(bf16)

    pl.semaphore_wait(barrier, groups + members - 2)

    def gram_copy(step):
        return pltpu.make_async_remote_copy(
            src_ref=gram_slots.at[st],
            dst_ref=gram_slots.at[st],
            send_sem=gram_send,
            recv_sem=gram_recv,
            device_id=(me, shifted(st, step, members)),
            device_id_type=MESH,
        )

    for step in far_members:
        gram_copy(step).start()

    def send_block(buffer, slots, owner, slot, send_sem, recv_sem):
        chip = owner_chip(owner, core, owners, groups)

        @pl.when(chip != me)
        def _():
            pltpu.make_async_remote_copy(
                src_ref=buffer.at[owner],
                dst_ref=slots.at[slot],
                send_sem=send_sem,
                recv_sem=recv_sem,
                device_id=(chip, st),
                device_id_type=MESH,
            ).start()

        @pl.when(chip == me)
        def _():
            slots[slot] = buffer[owner]

    span = groups // CHUNKS

    def send_observed(step):
        owner = lax.rem(first + around(step, owners), owners)
        offset = lax.rem(owner_chip(owner, core, owners, groups) - me + groups, groups)
        rank = far_rank(offset, groups)
        send_block(send_a, recv_a, owner, rank, a_send, a_recv.at[rank // span])

    early = owners // 2

    @pl.loop(0, early)
    def _(step):
        send_observed(step)

    others = gram_slots.at[pl.ds(0, members - 1)]
    pltpu.make_async_copy(others, others, gram_recv).wait()
    total = gram_slots[0]
    for member in range(1, members):
        total = total + gram_slots[member]
    total = jnp.broadcast_to(jnp.sum(total, axis=1, keepdims=True), total.shape)
    factor = {}
    inverse = []
    for row in range(elements):
        for col in range(row + 1):
            at = pair_at[row, col]
            running = total[at : at + 1, :]
            for mid in range(col):
                running = running - factor[row, mid] * factor[col, mid]
            if row == col:
                root = jnp.sqrt(running)
                inverse.append(1.0 / root)
            else:
                factor[row, col] = running * inverse[col]
    factor = {at: jnp.broadcast_to(value, (UNITS, LANES)) for at, value in factor.items()}
    inverse = [jnp.broadcast_to(value, (UNITS, LANES)) for value in inverse]

    @pl.loop(0, owners)
    def _(step):
        owner = lax.rem(first + around(step, owners), owners)
        forward = []
        for row in range(elements):
            running = bands_b[rows_of(row, owner), :]
            for mid in range(row):
                running = running - factor[row, mid] * forward[mid]
            forward.append(running * inverse[row])
        answer = [None] * elements
        for row in reversed(range(elements)):
            running = forward[row]
            for mid in range(row + 1, elements):
                running = running - factor[mid, row] * answer[mid]
            answer[row] = running * inverse[row]
        for pair in range(elements // 2):
            tile = jnp.concatenate([answer[2 * pair], answer[2 * pair + 1]], axis=0)
            send_b[owner, 2 * UNITS * pair : 2 * UNITS * (pair + 1), :] = tile.astype(bf16)
        send_block(send_b, recv_b, owner, me, b_send, b_recv)

    @pl.loop(early, owners)
    def _(step):
        send_observed(step)

    loads[4].wait()
    loads[5].wait()
    lane_id = lax.broadcasted_iota(jnp.int32, (cand_count, LANES), 1)
    node_id = lax.broadcasted_iota(jnp.int32, (cand_count, nodes), 1)
    eye = lax.broadcasted_iota(jnp.int32, (cand_count, cand_count), 0) == (
        lax.broadcasted_iota(jnp.int32, (cand_count, cand_count), 1)
    )
    slot_values = slot_ref[...].astype(f32)
    lane_rows = []
    for event in range(events):
        wanted = jnp.where(eye, cand_ref[event : event + 1, :].astype(f32), 0.0)
        wanted = jnp.sum(wanted, axis=1, keepdims=True)
        chosen = jnp.where(node_id.astype(f32) == wanted, slot_values, 0.0)
        lane_rows.append(jnp.sum(chosen, axis=1, keepdims=True))

    def spread(wide, target, count, height):
        @pl.loop(0, UNITS)
        def _(unit):
            lanes = pl.ds(pl.multiple_of(unit * LANES, LANES), LANES)
            for row in range(count):
                picked = wide[pl.ds(row * UNITS + unit, height, stride=count * UNITS), :]
                target[row * height : (row + 1) * height, lanes] = picked.astype(bf16)

    @pl.when(is_owner)
    def _():
        mixed[...] = jnp.zeros_like(mixed)
        arrived = recv_b.at[pl.ds(0, groups - 1)]
        pltpu.make_async_copy(arrived, arrived, b_recv).wait()
        wide_b[0 : groups * elements * UNITS, :] = (
            recv_b[...].astype(f32).reshape(groups * elements * UNITS, LANES)
        )
        spread(wide_b, matrix_b, elements, groups)
        for chunk in range(CHUNKS):
            start, stop = chunk * span, (chunk + 1) * span
            remote = min(stop, groups - 1)
            arrived = recv_a.at[pl.ds(start, remote - start)]
            pltpu.make_async_copy(arrived, arrived, a_recv.at[chunk]).wait()
            wide_a[0 : span * events * UNITS, :] = (
                recv_a[start:stop].astype(f32).reshape(span * events * UNITS, LANES)
            )
            spread(wide_a, matrix_a, events, span)
            products = lax.dot_general(
                matrix_a[...],
                matrix_b[...],
                (((1,), (1,)), ((), ())),
                preferred_element_type=f32,
            )
            for tile in range(elements * nodes // LANES):
                for event in range(events):
                    mixed[pl.ds(tile * events + event, span, stride=16), :] = products[
                        event * span : (event + 1) * span, tile * LANES : (tile + 1) * LANES
                    ]
            parts_out[start:stop] = (
                mixed[0 : span * 16, :].astype(bf16).reshape(span, 16, LANES)
            )

            @pl.loop(start, remote)
            def _(rank):
                peer = lax.rem(me - far_offset(rank, groups) + groups, groups)
                pltpu.make_async_remote_copy(
                    src_ref=parts_out.at[rank],
                    dst_ref=parts_in.at[my_owner],
                    send_sem=c_send,
                    recv_sem=c_recv,
                    device_id=(peer, st),
                    device_id_type=MESH,
                ).start()

        parts_in[my_owner] = parts_out[groups - 1]

    @pl.when(is_owner)
    def _():
        arrived = parts_in.at[pl.ds(0, owners - 1)]
        pltpu.make_async_copy(arrived, arrived, c_recv).wait()

    @pl.when(jnp.logical_not(is_owner))
    def _():
        arrived = parts_in.at[pl.ds(0, owners)]
        pltpu.make_async_copy(arrived, arrived, c_recv).wait()

    sum_slots[st] = jnp.sum(parts_in[...].astype(f32), axis=0)

    for step in far_members:
        pltpu.make_async_remote_copy(
            src_ref=sum_slots.at[st],
            dst_ref=sum_slots.at[st],
            send_sem=s_send,
            recv_sem=s_recv,
            device_id=(me, shifted(st, step, members)),
            device_id_type=MESH,
        ).start()

    others = sum_slots.at[pl.ds(0, members - 1)]
    pltpu.make_async_copy(others, others, s_recv).wait()
    moments = sum_slots[0]
    for member in range(1, members):
        moments = moments + sum_slots[member]

    lane_f = lane_id.astype(f32)
    out_lane = lax.broadcasted_iota(jnp.int32, (cand_count, LANES), 1)
    per_tile = LANES // nodes
    result = jnp.zeros((cand_count, LANES), f32)
    for event in range(events):
        for element in range(elements):
            tile, part = element // per_tile, element % per_tile
            line = moments[tile * events + event : tile * events + event + 1, :]
            mask = lane_f == lane_rows[event] + float(part * nodes)
            value = jnp.sum(jnp.where(mask, line, 0.0), axis=1, keepdims=True)
            result = jnp.where(out_lane == element * events + event, value, result)
    result = jnp.concatenate([result, jnp.zeros((LANES - cand_count, LANES), f32)], axis=0).T
    for element in range(elements):
        rows = result[element * events : (element + 1) * events, :cand_count]
        out_ref[element] = rows

    pltpu.make_async_copy(others, others, s_send).wait()
    sent = gram_slots.at[pl.ds(0, members - 1)]
    pltpu.make_async_copy(sent, sent, gram_send).wait()

    @pl.when(is_owner)
    def _():
        for buffer, sem in ((send_a, a_send), (send_b, b_send), (parts_out, c_send)):
            sent = buffer.at[pl.ds(0, buffer.shape[0] - 1)]
            pltpu.make_async_copy(sent, sent, sem).wait()

    @pl.when(jnp.logical_not(is_owner))
    def _():
        for buffer, sem in ((send_a, a_send), (send_b, b_send)):
            pltpu.make_async_copy(buffer, buffer, sem).wait()


def shards(records, store, taper, candidates, node_slot):
    groups, members = lax.axis_size("ev"), lax.axis_size("st")
    events, stations, comps, samples = records.shape
    elements = store.shape[1]
    traces = stations * comps
    bins = 2 * taper.shape[0]
    owners = traces * bins // (UNITS * LANES)
    cand_count = candidates.shape[1]
    nodes = node_slot.shape[0]
    dims = (groups, members, events, elements, traces, owners, cand_count, nodes)
    units = traces * (bins // LANES)
    f32, bf16 = jnp.float32, jnp.bfloat16
    table = jnp.asarray(band_table(samples, taper.shape[0]))
    rows_a, rows_b = events * UNITS, elements * UNITS
    result = pl.pallas_call(
        functools.partial(kernel, dims),
        out_shape=pltpu.VMEM((elements, events, cand_count), f32),
        in_specs=[pl.BlockSpec(memory_space=pltpu.HBM)] * 6,
        out_specs=pl.BlockSpec(memory_space=pltpu.VMEM),
        scratch_shapes=[
            pltpu.VMEM((traces, events, samples), bf16),
            pltpu.VMEM((elements * stations, comps, samples), bf16),
            pltpu.VMEM((samples, bins), bf16),
            pltpu.VMEM((1, taper.shape[0]), f32),
            pltpu.VMEM((events, cand_count), jnp.int32),
            pltpu.VMEM((1, nodes), jnp.int32),
            pltpu.VMEM((elements * traces * (bins // LANES), LANES), f32),
            pltpu.VMEM((events * units, LANES), f32),
            pltpu.VMEM((elements * units, LANES), f32),
            pltpu.VMEM((owners, rows_a, LANES), bf16),
            pltpu.VMEM((owners, rows_b, LANES), bf16),
            pltpu.VMEM((groups, rows_a, LANES), bf16),
            pltpu.VMEM((groups, rows_b, LANES), bf16),
            pltpu.VMEM(((groups // CHUNKS + 1) * rows_a, LANES), f32),
            pltpu.VMEM(((groups + 1) * rows_b, LANES), f32),
            pltpu.VMEM((groups // CHUNKS * events, UNITS * LANES), bf16),
            pltpu.VMEM((elements * groups, UNITS * LANES), bf16),
            pltpu.VMEM(((groups // CHUNKS + 1) * 16, LANES), f32),
            pltpu.VMEM((groups, 16, LANES), bf16),
            pltpu.VMEM((owners, 16, LANES), bf16),
            pltpu.VMEM((members, 24, LANES), f32),
            pltpu.VMEM((members, 16, LANES), f32),
            pltpu.SemaphoreType.DMA((6,)),
        ]
        + [pltpu.SemaphoreType.DMA] * 3
        + [pltpu.SemaphoreType.DMA((CHUNKS,))]
        + [pltpu.SemaphoreType.DMA] * 6,
        compiler_params=pltpu.CompilerParams(
            collective_id=0, has_side_effects=True, vmem_limit_bytes=54 * 1024 * 1024
        ),
    )(
        records.transpose(1, 2, 0, 3).reshape(traces, events, samples),
        store.reshape(elements * stations, comps, samples),
        table,
        taper.reshape(1, -1),
        candidates,
        node_slot.reshape(1, -1),
    )
    return result.transpose(1, 2, 0)


def solution(mesh):
    return jax.shard_map(
        shards,
        mesh=mesh,
        in_specs=(
            P("ev", "st", None, None),
            P("ev", None, "st", None, None),
            P(),
            P("ev", None),
            P(),
        ),
        out_specs=P("ev", None, None),
        check_vma=False,
    )
```
